32 devices in a mesh: dp: 4 (over z), seq: 8 (over y, x, core).
Axes of the slice: x: 2, y: 2, z: 4, core: 2. Of those that a mesh axis runs over, the one named last changes fastest.
Arguments:
- tokens: bfloat16 [32, 1024, 1152], P('dp', 'seq'), may hold values from -6 to 6
- key_mask: int32 [32, 1024], P('dp'), may hold values from 0 to 1, as said below
- cotangent: bfloat16 [32, 1024, 1152], P('dp', 'seq'), may hold values from -6 to 6
- qkv_weight: bfloat16 [1152, 3456], P('dp'), may hold values from -0.1875 to 0.1875
- output_weight: bfloat16 [1152, 1152], P('dp'), may hold values from -0.75 to 0.75
- expand_weight: bfloat16 [1152, 4304], P('dp'), may hold values from -0.1875 to 0.1875
- contract_weight: bfloat16 [1152, 4304], P('dp'), may hold values from -0.09375 to 0.09375
- norm1_gain: bfloat16 [1152], P('dp'), may hold values from 0.5 to 1.5
- norm1_bias: bfloat16 [1152], P('dp'), may hold values from -3 to 3
- query_bias: bfloat16 [1152], P('dp'), may hold values from -3 to 3
- value_bias: bfloat16 [1152], P('dp'), may hold values from -3 to 3
- output_bias: bfloat16 [1152], P('dp'), may hold values from -3 to 3
- norm2_gain: bfloat16 [1152], P('dp'), may hold values from 0.5 to 1.5
- norm2_bias: bfloat16 [1152], P('dp'), may hold values from -3 to 3
- expand_bias: bfloat16 [4304], P('dp'), may hold values from -3 to 3
- contract_bias: bfloat16 [1152], P('dp'), may hold values from -3 to 3
Outputs:
- layer_out: bfloat16 [32, 1024, 1152], P('dp', 'seq')
- input_grad: bfloat16 [32, 1024, 1152], P('dp', 'seq')
- qkv_weight_grad: float32 [1152, 3456], P('dp')
- output_weight_grad: float32 [1152, 1152], P('dp')
- expand_weight_grad: float32 [1152, 4304], P('dp')
- contract_weight_grad: float32 [1152, 4304], P('dp')
- norm1_gain_grad: float32 [1152], P('dp')
- norm1_bias_grad: float32 [1152], P('dp')
- query_bias_grad: float32 [1152], P('dp')
- value_bias_grad: float32 [1152], P('dp')
- output_bias_grad: float32 [1152], P('dp')
- norm2_gain_grad: float32 [1152], P('dp')
- norm2_bias_grad: float32 [1152], P('dp')
- expand_bias_grad: float32 [4304], P('dp')
- contract_bias_grad: float32 [1152], P('dp')
The draws below stay inside these ranges and needn't reach their ends.
Inputs may be any that keep to these rules, and one draw needn't show every extreme that they name: `key_mask`: each image's row holds ones at its first positions and zeros after them; an image has between half of 1024 and 961 ones, and among the 8 images of each index of dp one has exactly 961.
All inputs are finite; a program needn't handle non-finite values.
Results may differ from the reference program's by a relative error of at most 0.013.
Values may be sent and summed in bfloat16 or wider, within the bound.
A program may use at most 384 MiB of HBM per device.

```python
import math
import jax
import jax.numpy as jnp
from jax import lax

D = 1152
HEADS = 16
HEAD_DIM = 72
FF = 4304
LENGTH = 1024
VALID = 961
IMG_DEV = 8
IMAGES = 32


def draw_key_mask(key, part):
    key = jax.random.fold_in(key, 11)
    key_length, key_choose = jax.random.split(key)
    lengths = jax.random.randint(key_length, (IMAGES,), LENGTH // 2, VALID + 1)
    pick_rows = jax.random.randint(key_choose, (IMAGES // IMG_DEV,), 0, IMG_DEV)
    image_index = jnp.arange(IMAGES)
    chosen = pick_rows[image_index // IMG_DEV]
    lengths = jnp.where(image_index % IMG_DEV == chosen, VALID, lengths)
    return (jnp.arange(LENGTH)[None, :] < lengths[:, None]).astype(jnp.int32)


def steps_of(key, shape, cuts, least, largest):
    factor_of = 1.0
    for position, blocks in cuts:
        steps = jax.random.uniform(jax.random.fold_in(jax.random.fold_in(key, 6), position), (blocks,), jnp.float32, least / len(cuts), largest / len(cuts))
        factor_of = factor_of * jnp.repeat(jnp.exp(steps), shape[position] // blocks).reshape((-1,) + (1,) * (len(shape) - 1 - position))
    return factor_of


def noise(rng, dims, width, limit, shards=(), dtype=jnp.bfloat16):
    values = jax.random.normal(rng, dims, jnp.float32) * width
    if len(shards) > 0:
        values = steps_of(rng, dims, shards, -0.22, 0.18) * values
    return jnp.clip(values, min=-limit, max=limit).astype(dtype)


def setup_inputs(seed: int = 0) -> dict:
    seeds = jax.random.split(jax.random.key(seed), 17)
    return {
        "tokens": noise(seeds[0], (IMAGES, LENGTH, D), 1.0, 6.0, ((0, 4), (1, 8))),
        "key_mask": draw_key_mask(jax.random.fold_in(seeds[16], 71), 0),
        "cotangent": noise(seeds[2], (IMAGES, LENGTH, D), 1.0, 6.0, ((0, 4), (1, 8))),
        "qkv_weight": noise(seeds[3], (D, 3 * D), D ** -0.5, 0.1875, ((0, 4),)),
        "output_weight": noise(seeds[4], (D, D), (D // 16) ** -0.5, 0.75, ((0, 4),)),
        "expand_weight": noise(seeds[5], (D, FF), D ** -0.5, 0.1875, ((0, 4),)),
        "contract_weight": noise(seeds[6], (D, FF), FF ** -0.5, 0.09375, ((0, 4),)),
        "norm1_gain": jnp.clip(1.0 + 0.1 * jax.random.normal(seeds[7], (D,), jnp.float32), 0.5, 1.5).astype(jnp.bfloat16),
        "norm1_bias": noise(seeds[8], (D,), 0.5, 3.0, ((0, 4),)),
        "query_bias": noise(seeds[9], (D,), 0.5, 3.0, ((0, 4),)),
        "value_bias": noise(seeds[10], (D,), 0.5, 3.0, ((0, 4),)),
        "output_bias": noise(seeds[11], (D,), 0.5, 3.0, ((0, 4),)),
        "norm2_gain": jnp.clip(1.0 + 0.1 * jax.random.normal(seeds[12], (D,), jnp.float32), 0.5, 1.5).astype(jnp.bfloat16),
        "norm2_bias": noise(seeds[13], (D,), 0.5, 3.0, ((0, 4),)),
        "expand_bias": noise(seeds[14], (FF,), 0.5, 3.0, ((0, 4),)),
        "contract_bias": noise(seeds[15], (D,), 0.5, 3.0, ((0, 4),)),
    }


EPSILON = 1e-06
GELU_COEF = 0.7978845608028654
NEGATIVE = -1000000000.0

@jax.custom_vjp
def low(v):
    return lax.optimization_barrier(v.astype(jnp.bfloat16)).astype(jnp.float32)

@jax.custom_vjp
def low_back(v):
    return v

def low_keep(v):
    return (low(v), None)

def low_pass(kept, grad):
    return (grad,)

def back_keep(v):
    return (v, None)

def back_low(kept, grad):
    return (low(grad),)
low.defvjp(low_keep, low_pass)
low_back.defvjp(back_keep, back_low)

def layer_norm(values, scale_gain, shift_bias):
    center = values - lax.optimization_barrier(jnp.mean(values, axis=-1, keepdims=True))
    spread = lax.optimization_barrier(jnp.mean(center * center, axis=-1, keepdims=True))
    return center * lax.rsqrt(spread + EPSILON) * scale_gain + shift_bias

def gelu_tanh(values):
    return 0.5 * values * (1.0 + jnp.tanh(GELU_COEF * (values + 0.044715 * values * values * values)))

def matmul_high(left_mat, right_mat):
    return jnp.matmul(left_mat, right_mat, precision=lax.Precision.HIGHEST)

def forward(inputs, weights, key_valid):
    qkv_weight, output_weight, expand_weight, contract_weight, norm1_gain, norm1_bias, query_bias, value_bias, output_bias, norm2_gain, norm2_bias, expand_bias, contract_bias = weights
    images_here = inputs.shape[0]
    normed = low(layer_norm(inputs, norm1_gain, norm1_bias))
    bias_three = jnp.concatenate([query_bias, jnp.zeros_like(query_bias), value_bias])
    packed = low_back(low(matmul_high(normed, qkv_weight) + bias_three))
    packed = packed.reshape(images_here, LENGTH, 3, HEADS, HEAD_DIM)
    query_heads = packed[:, :, 0]
    key_heads = packed[:, :, 1]
    value_heads = packed[:, :, 2]
    scores = jnp.einsum('bqhd,bkhd->bhqk', query_heads, key_heads, precision=lax.Precision.HIGHEST)
    scores = low_back(scores * HEAD_DIM ** (-0.5))
    scores = jnp.where(key_valid[:, None, None, :], scores, NEGATIVE)
    soft_probs = low(jax.nn.softmax(scores, axis=-1))
    context = jnp.einsum('bhqk,bkhd->bqhd', soft_probs, value_heads, precision=lax.Precision.HIGHEST)
    context = low_back(low(context.reshape(images_here, LENGTH, D)))
    branch = low_back(matmul_high(context, output_weight) + output_bias)
    middle = inputs + branch
    normed_two = low(layer_norm(middle, norm2_gain, norm2_bias))
    hidden_pre = low_back(matmul_high(normed_two, expand_weight) + expand_bias)
    activated = low(gelu_tanh(hidden_pre))
    mlp_out = low_back(matmul_high(activated, contract_weight.T) + contract_bias)
    return middle + mlp_out

def reference(tokens, key_mask, cotangent, qkv_weight, output_weight, expand_weight, contract_weight, norm1_gain, norm1_bias, query_bias, value_bias, output_bias, norm2_gain, norm2_bias, expand_bias, contract_bias):
    params = tuple((weight_arg.astype(jnp.float32) for weight_arg in (qkv_weight, output_weight, expand_weight, contract_weight, norm1_gain, norm1_bias, query_bias, value_bias, output_bias, norm2_gain, norm2_bias, expand_bias, contract_bias)))
    images_total = tokens.shape[0]
    group_size = math.gcd(images_total, 4)
    groups = images_total // group_size
    inputs_all = tokens.astype(jnp.float32).reshape(groups, group_size, LENGTH, D)
    grads_in = cotangent.astype(jnp.float32).reshape(groups, group_size, LENGTH, D)
    valid_all = (key_mask > 0).reshape(groups, group_size, LENGTH)

    def group_step(accum_grads, batch_item):
        inputs_group, grads_group, valid_group = batch_item

        def apply_layer(inputs_here, params_here):
            return forward(inputs_here, params_here, valid_group)
        outputs_group, pullback = jax.vjp(apply_layer, inputs_group, params)
        input_part, param_part = pullback(grads_group)
        accum_grads = jax.tree.map(lambda first_term, second_term: first_term + second_term, accum_grads, param_part)
        return (accum_grads, (outputs_group.astype(jnp.bfloat16), input_part.astype(jnp.bfloat16)))
    zero_grads = tuple((jnp.zeros_like(weight_arg) for weight_arg in params))
    summed, (outputs_all, input_all) = lax.scan(group_step, zero_grads, (inputs_all, grads_in, valid_all))
    layer_out = outputs_all.reshape(tokens.shape)
    input_grad = input_all.reshape(tokens.shape)
    return (layer_out, input_grad, summed[0], summed[1], summed[2], summed[3], summed[4], summed[5], summed[6], summed[7], summed[8], summed[9], summed[10], summed[11], summed[12])
```

```python
import functools

import jax
import jax.numpy as jnp
from jax import lax
from jax.experimental import pallas as pl
from jax.experimental.pallas import tpu as pltpu
from jax.sharding import PartitionSpec as P

HEAD_DIM = 72


EPSILON = 1e-06
GELU_COEF = 0.7978845608028654
NEGATIVE = -1000000000.0


def layer_norm(values, scale_gain, shift_bias):
    center = values - jnp.mean(values, axis=-1, keepdims=True)
    spread = jnp.mean(center * center, axis=-1, keepdims=True)
    return center * lax.rsqrt(spread + EPSILON) * scale_gain + shift_bias


def gelu_tanh(values):
    return (
        0.5 * values * (1.0 + jnp.tanh(GELU_COEF * (values + 0.044715 * values * values * values)))
    )


def attend_scores(query_heads, key_heads, key_valid):
    raw_scores = jnp.einsum(
        "bqhd,bkhd->bhqk", query_heads, key_heads, preferred_element_type=jnp.float32
    )
    raw_scores = raw_scores * HEAD_DIM ** (-0.5)
    return jnp.where(key_valid[:, None, None, :], raw_scores, NEGATIVE)


def shards_general(
    tokens,
    key_mask,
    cotangent,
    qkv_weight,
    output_weight,
    expand_weight,
    contract_weight,
    norm1_gain,
    norm1_bias,
    query_bias,
    value_bias,
    output_bias,
    norm2_gain,
    norm2_bias,
    expand_bias,
    contract_bias,
):
    images_here, slice_len, feature_width = tokens.shape
    seq_count = lax.axis_size("seq")
    total_rows = images_here * slice_len
    full_length = slice_len * seq_count
    local_width = feature_width // seq_count
    local_heads = local_width // HEAD_DIM
    row_dims = (((0,), (0,)), ((), ()))
    col_dims = (((1,), (1,)), ((), ()))
    (
        qkv_full,
        output_full,
        expand_full,
        contract_full,
        gain_one,
        shift_one,
        query_shift,
        value_shift,
        output_shift,
        gain_two,
        shift_two,
        expand_shift,
        contract_shift,
    ) = (
        lax.all_gather(qkv_weight, "dp", axis=0, tiled=True),
        lax.all_gather(output_weight, "dp", axis=0, tiled=True),
        lax.all_gather(expand_weight, "dp", axis=0, tiled=True),
        lax.all_gather(contract_weight, "dp", axis=0, tiled=True),
        lax.all_gather(norm1_gain, "dp", axis=0, tiled=True),
        lax.all_gather(norm1_bias, "dp", axis=0, tiled=True),
        lax.all_gather(query_bias, "dp", axis=0, tiled=True),
        lax.all_gather(value_bias, "dp", axis=0, tiled=True),
        lax.all_gather(output_bias, "dp", axis=0, tiled=True),
        lax.all_gather(norm2_gain, "dp", axis=0, tiled=True),
        lax.all_gather(norm2_bias, "dp", axis=0, tiled=True),
        lax.all_gather(expand_bias, "dp", axis=0, tiled=True),
        lax.all_gather(contract_bias, "dp", axis=0, tiled=True),
    )
    inputs = tokens.reshape(total_rows, feature_width).astype(jnp.float32)
    normed, norm_one_back = jax.vjp(
        layer_norm, inputs, gain_one.astype(jnp.float32), shift_one.astype(jnp.float32)
    )
    normed_low = normed.astype(jnp.bfloat16)
    bias_three = jnp.concatenate([query_shift, jnp.zeros_like(query_shift), value_shift]).astype(
        jnp.float32
    )
    packed = jnp.dot(normed_low, qkv_full, preferred_element_type=jnp.float32) + bias_three
    packed = packed.astype(jnp.bfloat16).reshape(images_here, slice_len, 3, feature_width)
    by_heads = lax.all_to_all(packed, "seq", split_axis=3, concat_axis=1, tiled=True)
    head_shape = (images_here, full_length, local_heads, HEAD_DIM)
    query_heads = by_heads[:, :, 0].reshape(head_shape)
    key_heads = by_heads[:, :, 1].reshape(head_shape)
    value_heads = by_heads[:, :, 2].reshape(head_shape)
    key_valid = key_mask > 0
    scores = attend_scores(query_heads, key_heads, key_valid)
    row_peak = jnp.max(scores, axis=-1, keepdims=True)
    raised = jnp.exp(scores - row_peak)
    totals = jnp.sum(raised, axis=-1, keepdims=True)
    soft_probs = raised / totals
    log_total = row_peak + jnp.log(totals)
    probs_low = soft_probs.astype(jnp.bfloat16)
    context = jnp.einsum(
        "bhqk,bkhd->bqhd", probs_low, value_heads, preferred_element_type=jnp.float32
    )
    context = context.reshape(images_here, full_length, local_width).astype(jnp.bfloat16)
    by_tokens = lax.all_to_all(context, "seq", split_axis=1, concat_axis=2, tiled=True)
    context_rows = by_tokens.reshape(total_rows, feature_width)
    branch = jnp.dot(
        context_rows, output_full, preferred_element_type=jnp.float32
    ) + output_shift.astype(jnp.float32)
    middle = inputs + branch
    normed_two, norm_two_back = jax.vjp(
        layer_norm, middle, gain_two.astype(jnp.float32), shift_two.astype(jnp.float32)
    )
    normed_two_low = normed_two.astype(jnp.bfloat16)
    hidden_pre = jnp.dot(
        normed_two_low, expand_full, preferred_element_type=jnp.float32
    ) + expand_shift.astype(jnp.float32)
    activated, gelu_back = jax.vjp(gelu_tanh, hidden_pre)
    activated_low = activated.astype(jnp.bfloat16)
    mlp_out = lax.dot_general(
        activated_low, contract_full, col_dims, preferred_element_type=jnp.float32
    )
    mlp_out = mlp_out + contract_shift.astype(jnp.float32)
    layer_out = (middle + mlp_out).astype(jnp.bfloat16).reshape(tokens.shape)
    qkv_back, output_back, expand_back, contract_back = (
        lax.all_gather(qkv_weight, "dp", axis=0, tiled=True),
        lax.all_gather(output_weight, "dp", axis=0, tiled=True),
        lax.all_gather(expand_weight, "dp", axis=0, tiled=True),
        lax.all_gather(contract_weight, "dp", axis=0, tiled=True),
    )
    upstream = cotangent.reshape(total_rows, feature_width).astype(jnp.float32)
    mlp_grad = cotangent.reshape(total_rows, feature_width)
    grad_contract_bias = jnp.sum(upstream, axis=0)
    grad_contract = lax.dot_general(
        mlp_grad, activated_low, row_dims, preferred_element_type=jnp.float32
    )
    act_grad = jnp.dot(mlp_grad, contract_back, preferred_element_type=jnp.float32)
    (pre_grad,) = gelu_back(act_grad)
    pre_low = pre_grad.astype(jnp.bfloat16)
    grad_expand_bias = jnp.sum(pre_low.astype(jnp.float32), axis=0)
    grad_expand = lax.dot_general(
        normed_two_low, pre_low, row_dims, preferred_element_type=jnp.float32
    )
    normed_two_grad = lax.dot_general(
        pre_low, expand_back, col_dims, preferred_element_type=jnp.float32
    )
    middle_part, grad_gain_two, grad_shift_two = norm_two_back(normed_two_grad)
    middle_grad = upstream + middle_part
    branch_low = middle_grad.astype(jnp.bfloat16)
    grad_output_bias = jnp.sum(branch_low.astype(jnp.float32), axis=0)
    grad_output = lax.dot_general(
        context_rows, branch_low, row_dims, preferred_element_type=jnp.float32
    )
    context_grad = lax.dot_general(
        branch_low, output_back, col_dims, preferred_element_type=jnp.float32
    )
    context_grad = context_grad.astype(jnp.bfloat16).reshape(images_here, slice_len, feature_width)
    grad_heads = lax.all_to_all(
        context_grad, "seq", split_axis=2, concat_axis=1, tiled=True
    ).reshape(head_shape)
    scores_again = attend_scores(query_heads, key_heads, key_valid)
    probs_again = jnp.exp(scores_again - log_total)
    probs_again_low = probs_again.astype(jnp.bfloat16)
    prob_grad = jnp.einsum(
        "bqhd,bkhd->bhqk", grad_heads, value_heads, preferred_element_type=jnp.float32
    )
    value_grad = jnp.einsum(
        "bhqk,bqhd->bkhd", probs_again_low, grad_heads, preferred_element_type=jnp.float32
    )
    row_dot = jnp.sum(probs_again * prob_grad, axis=-1, keepdims=True)
    score_low = (probs_again * (prob_grad - row_dot)).astype(jnp.bfloat16)
    query_grad = jnp.einsum(
        "bhqk,bkhd->bqhd", score_low, key_heads, preferred_element_type=jnp.float32
    ) * HEAD_DIM ** (-0.5)
    key_grad = jnp.einsum(
        "bhqk,bqhd->bkhd", score_low, query_heads, preferred_element_type=jnp.float32
    ) * HEAD_DIM ** (-0.5)
    stacked = jnp.stack([query_grad, key_grad, value_grad], axis=2)
    stacked = stacked.reshape(images_here, full_length, 3, local_width).astype(jnp.bfloat16)
    back_packed = lax.all_to_all(stacked, "seq", split_axis=1, concat_axis=3, tiled=True)
    packed_grad = back_packed.reshape(total_rows, 3 * feature_width)
    grad_query_bias = jnp.sum(packed_grad[:, :feature_width].astype(jnp.float32), axis=0)
    grad_value_bias = jnp.sum(packed_grad[:, 2 * feature_width :].astype(jnp.float32), axis=0)
    grad_qkv = lax.dot_general(
        normed_low, packed_grad, row_dims, preferred_element_type=jnp.float32
    )
    normed_grad = lax.dot_general(
        packed_grad, qkv_back, col_dims, preferred_element_type=jnp.float32
    )
    input_part, grad_gain_one, grad_shift_one = norm_one_back(normed_grad)
    input_grad = (middle_grad + input_part).astype(jnp.bfloat16).reshape(tokens.shape)
    shares = (
        lax.psum_scatter(grad_qkv, ("dp", "seq"), scatter_dimension=0, tiled=True),
        lax.psum_scatter(grad_output, ("dp", "seq"), scatter_dimension=0, tiled=True),
        lax.psum_scatter(grad_expand, ("dp", "seq"), scatter_dimension=0, tiled=True),
        lax.psum_scatter(grad_contract, ("dp", "seq"), scatter_dimension=0, tiled=True),
        lax.psum_scatter(grad_gain_one, ("dp", "seq"), scatter_dimension=0, tiled=True),
        lax.psum_scatter(grad_shift_one, ("dp", "seq"), scatter_dimension=0, tiled=True),
        lax.psum_scatter(grad_query_bias, ("dp", "seq"), scatter_dimension=0, tiled=True),
        lax.psum_scatter(grad_value_bias, ("dp", "seq"), scatter_dimension=0, tiled=True),
        lax.psum_scatter(grad_output_bias, ("dp", "seq"), scatter_dimension=0, tiled=True),
        lax.psum_scatter(grad_gain_two, ("dp", "seq"), scatter_dimension=0, tiled=True),
        lax.psum_scatter(grad_shift_two, ("dp", "seq"), scatter_dimension=0, tiled=True),
        lax.psum_scatter(grad_contract_bias, ("dp", "seq"), scatter_dimension=0, tiled=True),
    )
    summed = (
        lax.all_gather(shares[0].astype(jnp.bfloat16), "seq", axis=0, tiled=True).astype(
            jnp.float32
        ),
        lax.all_gather(shares[1].astype(jnp.bfloat16), "seq", axis=0, tiled=True).astype(
            jnp.float32
        ),
        lax.all_gather(shares[2].astype(jnp.bfloat16), "seq", axis=0, tiled=True).astype(
            jnp.float32
        ),
        lax.all_gather(shares[3].astype(jnp.bfloat16), "seq", axis=0, tiled=True).astype(
            jnp.float32
        ),
        lax.all_gather(shares[4].astype(jnp.bfloat16), "seq", axis=0, tiled=True).astype(
            jnp.float32
        ),
        lax.all_gather(shares[5].astype(jnp.bfloat16), "seq", axis=0, tiled=True).astype(
            jnp.float32
        ),
        lax.all_gather(shares[6].astype(jnp.bfloat16), "seq", axis=0, tiled=True).astype(
            jnp.float32
        ),
        lax.all_gather(shares[7].astype(jnp.bfloat16), "seq", axis=0, tiled=True).astype(
            jnp.float32
        ),
        lax.all_gather(shares[8].astype(jnp.bfloat16), "seq", axis=0, tiled=True).astype(
            jnp.float32
        ),
        lax.all_gather(shares[9].astype(jnp.bfloat16), "seq", axis=0, tiled=True).astype(
            jnp.float32
        ),
        lax.all_gather(shares[10].astype(jnp.bfloat16), "seq", axis=0, tiled=True).astype(
            jnp.float32
        ),
        lax.all_gather(shares[11].astype(jnp.bfloat16), "seq", axis=0, tiled=True).astype(
            jnp.float32
        ),
    )
    hidden_total = lax.psum(grad_expand_bias, ("dp", "seq"))
    share_rows = hidden_total.shape[0] // lax.axis_size("dp")
    expand_bias_part = lax.dynamic_slice_in_dim(
        hidden_total, lax.axis_index("dp") * share_rows, share_rows, 0
    )
    final = tuple(summed) + (expand_bias_part,)
    return (
        layer_out,
        input_grad,
        final[0],
        final[1],
        final[2],
        final[3],
        final[4],
        final[5],
        final[6],
        final[7],
        final[8],
        final[9],
        final[10],
        final[12],
        final[11],
    )


F32 = jnp.float32
BF16 = jnp.bfloat16
SCALE = HEAD_DIM ** (-0.5)
LOG2_E = 1.4426950408889634
MIB = 1024 * 1024
NN = (((1,), (0,)), ((), ()))
NT = (((1,), (1,)), ((), ()))
TN = (((0,), (0,)), ((), ()))


def mm(left, right, dims):
    return lax.dot_general(left, right, dims, preferred_element_type=F32)


def whole(shape):
    return pl.BlockSpec(shape, lambda *_: (0,) * len(shape))


def params(limit):
    return pltpu.CompilerParams(vmem_limit_bytes=limit * MIB)


def centred(values):
    center = values - jnp.mean(values, axis=-1, keepdims=True)
    rate = lax.rsqrt(jnp.mean(center * center, axis=-1, keepdims=True) + EPSILON)
    return center * rate, rate


def qkv_kernel(x_ref, gain_ref, shift_ref, weight_ref, bias_ref, packed_ref, normed_t_ref):
    rows = 128

    @pl.when(pl.program_id(0) == 0)
    def _():
        def part(i, carry):
            at = pl.ds(pl.multiple_of(i * rows, rows), rows)
            hat, _ = centred(x_ref[at, :].astype(F32))
            normed = (hat * gain_ref[...] + shift_ref[...]).astype(BF16)
            normed_t_ref[:, at] = normed.T
            return carry

        lax.fori_loop(0, x_ref.shape[0] // rows, part, 0)

    prod = mm(weight_ref[...], normed_t_ref[...], TN)
    packed_ref[...] = (prod + bias_ref[...]).astype(BF16)


def qkv_forward(x, gain, shift, weight, bias):
    tokens, width = x.shape
    total = weight.shape[1]
    step = 384
    return pl.pallas_call(
        qkv_kernel,
        grid=(total // step,),
        in_specs=[
            whole((tokens, width)),
            whole((1, width)),
            whole((1, width)),
            pl.BlockSpec((width, step), lambda i: (0, i)),
            pl.BlockSpec((step, 1), lambda i: (i, 0)),
        ],
        out_specs=[pl.BlockSpec((step, tokens), lambda i: (i, 0)), whole((width, tokens))],
        out_shape=[
            jax.ShapeDtypeStruct((total, tokens), BF16),
            jax.ShapeDtypeStruct((width, tokens), BF16),
        ],
        compiler_params=params(48),
        name="qkv_forward",
    )(x, gain, shift, weight, bias)


def heads_of(ref, head):
    return ref[...].astype(F32)[head * HEAD_DIM : (head + 1) * HEAD_DIM]


def attend_kernel(q_ref, k_ref, v_ref, mask_ref, raised_ref, context_ref, inverse_ref):
    tokens = q_ref.shape[1]
    chunk = 256
    for head in range(2):
        keys_t = heads_of(k_ref, head)
        keys = jnp.concatenate([keys_t, mask_ref[...]], axis=0).T.astype(BF16)
        queries_t = heads_of(q_ref, head)
        ones = jnp.ones((8, tokens), F32)
        queries_t = jnp.concatenate([queries_t, ones], axis=0).astype(BF16)
        values_t = heads_of(v_ref, head).astype(BF16)
        for c in range(tokens // chunk):
            at = slice(c * chunk, (c + 1) * chunk)
            scores = mm(keys, queries_t[:, at], NN)
            peak = jnp.max(scores, axis=0, keepdims=True)
            raised = jnp.exp2((scores - peak) * (SCALE * LOG2_E))
            inverse = 1.0 / jnp.sum(raised, axis=0, keepdims=True)
            low = raised.astype(BF16)
            raised_ref[head, :, at] = low
            inverse_ref[0, head : head + 1, at] = inverse
            context = mm(values_t, low, NN) * inverse
            context_ref[head * HEAD_DIM : (head + 1) * HEAD_DIM, at] = context


def attend_forward(packed, mask_rows):
    total, tokens = packed.shape
    pair = 2 * HEAD_DIM
    pairs = total // 3 // pair
    return pl.pallas_call(
        attend_kernel,
        grid=(pairs,),
        in_specs=[
            pl.BlockSpec((pair, tokens), lambda i: (i, 0)),
            pl.BlockSpec((pair, tokens), lambda i: (i + pairs, 0)),
            pl.BlockSpec((pair, tokens), lambda i: (i + 2 * pairs, 0)),
            whole((8, tokens)),
        ],
        out_specs=[
            pl.BlockSpec((2, tokens, tokens), lambda i: (i, 0, 0)),
            pl.BlockSpec((pair, tokens), lambda i: (i, 0)),
            pl.BlockSpec((1, 2, tokens), lambda i: (i, 0, 0)),
        ],
        out_shape=[
            jax.ShapeDtypeStruct((2 * pairs, tokens, tokens), BF16),
            jax.ShapeDtypeStruct((total // 3, tokens), F32),
            jax.ShapeDtypeStruct((pairs, 2, tokens), F32),
        ],
        compiler_params=params(48),
        name="attend_forward",
    )(packed, packed, packed, mask_rows)


def join_kernel(x_ref, context_ref, weight_ref, bias_ref, gain_ref, shift_ref, middle_ref, normed_ref):
    branch = mm(context_ref[...].astype(BF16), weight_ref[...], TN)
    middle = x_ref[...].astype(F32) + (branch + bias_ref[...])
    middle_ref[...] = middle
    hat, _ = centred(middle)
    normed_ref[...] = (hat * gain_ref[...] + shift_ref[...]).astype(BF16)


def join_forward(x, context_t, weight, bias, gain, shift):
    tokens, width = x.shape
    step = 256
    return pl.pallas_call(
        join_kernel,
        grid=(tokens // step,),
        in_specs=[
            pl.BlockSpec((step, width), lambda i: (i, 0)),
            pl.BlockSpec((width, step), lambda i: (0, i)),
            whole((width, width)),
            whole((1, width)),
            whole((1, width)),
            whole((1, width)),
        ],
        out_specs=[pl.BlockSpec((step, width), lambda i: (i, 0))] * 2,
        out_shape=[
            jax.ShapeDtypeStruct((tokens, width), F32),
            jax.ShapeDtypeStruct((tokens, width), BF16),
        ],
        compiler_params=params(48),
        name="join_forward",
    )(x, context_t, weight, bias, gain, shift)


def mlp_kernel(
    hidden_count,
    normed_ref,
    cot_ref,
    expand_ref,
    contract_ref,
    bias_ref,
    middle_ref,
    contract_bias_ref,
    gain_ref,
    out_ref,
    middle_grad_ref,
    expand_grad_ref,
    contract_grad_ref,
    expand_bias_grad_ref,
    sums_ref,
    normed_t_ref,
    cot_t_ref,
    out_acc_ref,
    back_acc_ref,
):
    index = pl.program_id(0)
    tokens, width = normed_ref.shape
    block = expand_ref.shape[1]
    rows = 128

    @pl.when(index == 0)
    def _():
        def part(i, carry):
            at = pl.ds(pl.multiple_of(i * rows, rows), rows)
            normed_t_ref[:, at] = normed_ref[at, :].T
            cot_t_ref[:, at] = cot_ref[at, :].T
            out_acc_ref[at, :] = jnp.zeros((rows, width), F32)
            back_acc_ref[at, :] = jnp.zeros((rows, width), F32)
            return carry

        lax.fori_loop(0, tokens // rows, part, 0)

    column = lax.broadcasted_iota(jnp.int32, (1, block), 1) + index * block
    kept = column < hidden_count
    expand = jnp.where(kept, expand_ref[...], jnp.zeros((), BF16))
    contract = jnp.where(kept, contract_ref[...], jnp.zeros((), BF16))
    bias = jnp.where(kept, bias_ref[...], 0.0)
    hidden = mm(normed_ref[...], expand, NN) + bias
    act_grad = mm(cot_ref[...], contract, NN)
    square = hidden * hidden
    tanh = jnp.tanh(hidden * (GELU_COEF + (GELU_COEF * 0.044715) * square))
    half = 0.5 + 0.5 * tanh
    activated = (hidden * half).astype(BF16)
    slope = half + (0.5 * hidden) * (1.0 - tanh * tanh) * (
        GELU_COEF + (3 * 0.044715 * GELU_COEF) * square
    )
    pre_grad = act_grad * slope
    pre_low = pre_grad.astype(BF16)
    expand_bias_grad_ref[...] = jnp.sum(pre_low.astype(F32), axis=0, keepdims=True)
    out_acc_ref[...] += mm(activated, contract, NT)
    contract_grad_ref[...] = mm(cot_t_ref[...], activated, NN).astype(BF16)
    expand_grad_ref[...] = mm(normed_t_ref[...], pre_low, NN).astype(BF16)
    back_acc_ref[...] += mm(pre_low, expand, NT)

    @pl.when(index == pl.num_programs(0) - 1)
    def _():
        def part(i, sums):
            at = pl.ds(pl.multiple_of(i * rows, rows), rows)
            middle = middle_ref[at, :]
            cot = cot_ref[at, :].astype(F32)
            out_ref[at, :] = (middle + (out_acc_ref[at, :] + contract_bias_ref[...])).astype(BF16)
            hat, rate = centred(middle)
            grad = back_acc_ref[at, :]
            scaled = grad * gain_ref[...]
            mean_one = jnp.mean(scaled, axis=-1, keepdims=True)
            mean_two = jnp.mean(scaled * hat, axis=-1, keepdims=True)
            middle_grad = cot + rate * (scaled - mean_one - hat * mean_two)
            middle_grad_ref[at, :] = middle_grad
            low = middle_grad.astype(BF16).astype(F32)
            terms = (grad * hat, grad, low, cot)
            return tuple(
                total + jnp.sum(term, axis=0, keepdims=True) for total, term in zip(sums, terms)
            )

        zero = jnp.zeros((1, width), F32)
        sums = lax.fori_loop(0, tokens // rows, part, (zero,) * 4)
        for place, total in enumerate(sums):
            sums_ref[place : place + 1, :] = total


def mlp_both(normed, cot, expand, contract, bias, middle, contract_bias, gain):
    tokens, width = normed.shape
    hidden_count = expand.shape[1]
    block = 256
    steps = -(-hidden_count // block)
    columns = pl.BlockSpec((width, block), lambda i: (0, i))
    return pl.pallas_call(
        functools.partial(mlp_kernel, hidden_count),
        grid=(steps,),
        in_specs=[
            whole((tokens, width)),
            whole((tokens, width)),
            columns,
            columns,
            pl.BlockSpec((1, block), lambda i: (0, i)),
            whole((tokens, width)),
            whole((1, width)),
            whole((1, width)),
        ],
        out_specs=[
            whole((tokens, width)),
            whole((tokens, width)),
            columns,
            columns,
            pl.BlockSpec((1, block), lambda i: (0, i)),
            whole((8, width)),
        ],
        out_shape=[
            jax.ShapeDtypeStruct((tokens, width), BF16),
            jax.ShapeDtypeStruct((tokens, width), F32),
            jax.ShapeDtypeStruct((width, hidden_count), BF16),
            jax.ShapeDtypeStruct((width, hidden_count), BF16),
            jax.ShapeDtypeStruct((1, hidden_count), F32),
            jax.ShapeDtypeStruct((8, width), F32),
        ],
        scratch_shapes=[
            pltpu.VMEM((width, tokens), BF16),
            pltpu.VMEM((width, tokens), BF16),
            pltpu.VMEM((tokens, width), F32),
            pltpu.VMEM((tokens, width), F32),
        ],
        compiler_params=params(60),
        name="mlp_both",
    )(normed, cot, expand, contract, bias, middle, contract_bias, gain)


def branch_kernel(middle_grad_ref, context_ref, weight_ref, context_grad_ref, weight_grad_ref, total_ref):
    index = pl.program_id(0)
    low = middle_grad_ref[...].astype(BF16)
    context_grad_ref[...] = mm(weight_ref[...], low, NT).astype(BF16)
    part = mm(context_ref[...].astype(BF16), low, NN)

    @pl.when(index == 0)
    def _():
        total_ref[...] = part

    @pl.when(index > 0)
    def _():
        total_ref[...] += part

    @pl.when(index == pl.num_programs(0) - 1)
    def _():
        weight_grad_ref[...] = total_ref[...].astype(BF16)


def branch_back(middle_grad, context_t, weight):
    tokens, width = middle_grad.shape
    step = 256
    return pl.pallas_call(
        branch_kernel,
        grid=(tokens // step,),
        in_specs=[
            pl.BlockSpec((step, width), lambda i: (i, 0)),
            pl.BlockSpec((width, step), lambda i: (0, i)),
            whole((width, width)),
        ],
        out_specs=[pl.BlockSpec((width, step), lambda i: (0, i)), whole((width, width))],
        out_shape=[
            jax.ShapeDtypeStruct((width, tokens), BF16),
            jax.ShapeDtypeStruct((width, width), BF16),
        ],
        scratch_shapes=[pltpu.VMEM((width, width), F32)],
        compiler_params=params(48),
        name="branch_back",
    )(middle_grad, context_t, weight)


def attend_back_kernel(
    q_ref, k_ref, v_ref, grad_ref, context_ref, inverse_ref, raised_ref, packed_grad_ref
):
    tokens = q_ref.shape[1]
    chunk = 256
    for head in range(2):
        span = slice(head * HEAD_DIM, (head + 1) * HEAD_DIM)
        keys_t = heads_of(k_ref, head).astype(BF16)
        queries_t = heads_of(q_ref, head).astype(BF16)
        values = heads_of(v_ref, head).T.astype(BF16)
        grad = heads_of(grad_ref, head) * inverse_ref[0, head : head + 1, :]
        grad_low = grad.astype(BF16)
        drop = jnp.sum(grad_low.astype(F32) * context_ref[span, :], axis=0, keepdims=True)
        key_grad = jnp.zeros((HEAD_DIM, tokens), F32)
        value_grad = jnp.zeros((HEAD_DIM, tokens), F32)
        for c in range(tokens // chunk):
            at = slice(c * chunk, (c + 1) * chunk)
            raised = raised_ref[head, :, at]
            prob_grad = mm(values, grad_low[:, at], NN)
            score = (raised.astype(F32) * (prob_grad - drop[:, at])).astype(BF16)
            packed_grad_ref[0, span, at] = (mm(keys_t, score, NN) * SCALE).astype(BF16)
            key_grad += mm(queries_t[:, at], score, NT)
            value_grad += mm(grad_low[:, at], raised, NT)
        packed_grad_ref[1, span, :] = (key_grad * SCALE).astype(BF16)
        packed_grad_ref[2, span, :] = value_grad.astype(BF16)


def attend_back(packed, context_grad, context_t, inverse, raised):
    total, tokens = packed.shape
    pair = 2 * HEAD_DIM
    width = total // 3
    pairs = width // pair
    one = pl.BlockSpec((pair, tokens), lambda i: (i, 0))
    return pl.pallas_call(
        attend_back_kernel,
        grid=(pairs,),
        in_specs=[
            one,
            pl.BlockSpec((pair, tokens), lambda i: (i + pairs, 0)),
            pl.BlockSpec((pair, tokens), lambda i: (i + 2 * pairs, 0)),
            one,
            one,
            pl.BlockSpec((1, 2, tokens), lambda i: (i, 0, 0)),
            pl.BlockSpec((2, tokens, tokens), lambda i: (i, 0, 0)),
        ],
        out_specs=pl.BlockSpec((3, pair, tokens), lambda i: (0, i, 0)),
        out_shape=jax.ShapeDtypeStruct((3, width, tokens), BF16),
        compiler_params=params(56),
        name="attend_back",
    )(packed, packed, packed, context_grad, context_t, inverse, raised)


def input_kernel(
    normed_t_ref,
    packed_grad_ref,
    weight_ref,
    x_ref,
    middle_grad_ref,
    gain_ref,
    input_grad_ref,
    weight_grad_ref,
    bias_grad_ref,
    sums_ref,
    back_ref,
):
    index = pl.program_id(0)
    tokens, width = x_ref.shape
    rows = 128
    packed_grad = packed_grad_ref[...]
    weight_grad_ref[...] = mm(normed_t_ref[...], packed_grad, NT).astype(BF16)
    bias_grad_ref[...] = jnp.sum(packed_grad.astype(F32), axis=1, keepdims=True)
    part = mm(weight_ref[...], packed_grad, NN)

    @pl.when(index == 0)
    def _():
        back_ref[...] = part

    @pl.when(index > 0)
    def _():
        back_ref[...] += part

    @pl.when(index == pl.num_programs(0) - 1)
    def _():
        def part_of(i, sums):
            at = pl.ds(pl.multiple_of(i * rows, rows), rows)
            hat, rate = centred(x_ref[at, :].astype(F32))
            grad = back_ref[:, at].T
            scaled = grad * gain_ref[...]
            mean_one = jnp.mean(scaled, axis=-1, keepdims=True)
            mean_two = jnp.mean(scaled * hat, axis=-1, keepdims=True)
            result = middle_grad_ref[at, :] + rate * (scaled - mean_one - hat * mean_two)
            input_grad_ref[at, :] = result.astype(BF16)
            terms = (grad * hat, grad)
            return tuple(
                total + jnp.sum(term, axis=0, keepdims=True) for total, term in zip(sums, terms)
            )

        zero = jnp.zeros((1, width), F32)
        sums = lax.fori_loop(0, tokens // rows, part_of, (zero,) * 2)
        for place, total in enumerate(sums):
            sums_ref[place : place + 1, :] = total


def input_back(normed_t, packed_grad, weight, x, middle_grad, gain):
    tokens, width = x.shape
    total = weight.shape[1]
    step = 384
    return pl.pallas_call(
        input_kernel,
        grid=(total // step,),
        in_specs=[
            whole((width, tokens)),
            pl.BlockSpec((step, tokens), lambda i: (i, 0)),
            pl.BlockSpec((width, step), lambda i: (0, i)),
            whole((tokens, width)),
            whole((tokens, width)),
            whole((1, width)),
        ],
        out_specs=[
            whole((tokens, width)),
            pl.BlockSpec((width, step), lambda i: (0, i)),
            pl.BlockSpec((step, 1), lambda i: (i, 0)),
            whole((8, width)),
        ],
        out_shape=[
            jax.ShapeDtypeStruct((tokens, width), BF16),
            jax.ShapeDtypeStruct((width, total), BF16),
            jax.ShapeDtypeStruct((total, 1), F32),
            jax.ShapeDtypeStruct((8, width), F32),
        ],
        scratch_shapes=[pltpu.VMEM((width, tokens), F32)],
        compiler_params=params(56),
        name="input_back",
    )(normed_t, packed_grad, weight, x, middle_grad, gain)


UNIT = 16
MESH_ID = pl.DeviceIdType.MESH


class Place:
    def __init__(self):
        self.depth = lax.axis_size("dp")
        self.z = lax.axis_index("dp")
        self.j = lax.axis_index("seq")
        self.core = self.j % 2
        self.x = (self.j // 2) % 2
        self.y = self.j // 4
        self.pos = self.j // 2

    def near(self, flip):
        other = self.j
        if flip & 1:
            other = other + 1 - 2 * self.core
        if flip & 2:
            other = other + 2 - 4 * self.x
        if flip & 4:
            other = other + 4 - 8 * self.y
        return other

    def plane(self, flip):
        return (self.z, self.near(flip))

    def pos_near(self, flip):
        return self.near(flip) // 2

    def line(self, step):
        return ((self.z + step) % self.depth, self.j)

    def from_line(self, step):
        return (self.z + self.depth - step) % self.depth


def greet(devices):
    barrier = pltpu.get_barrier_semaphore()
    for device in devices:
        pl.semaphore_signal(barrier, inc=1, device_id=device, device_id_type=MESH_ID)
    pl.semaphore_wait(barrier, len(devices))


class Links:
    def __init__(self, send_ref, recv_ref):
        self.send_ref, self.recv_ref, self.used = send_ref, recv_ref, 0

    def slot(self):
        self.used += 1
        return self.used - 1

    def copy(self, slot, source, target, device):
        return pltpu.make_async_remote_copy(
            src_ref=source,
            dst_ref=target,
            send_sem=self.send_ref.at[slot],
            recv_sem=self.recv_ref.at[slot],
            device_id=device,
            device_id_type=MESH_ID,
        )


def rows_of(ref, start, count):
    return ref.at[pl.ds(pl.multiple_of(start, UNIT), count), :]


class Gather:
    def __init__(self, here, links, shard_ref, full_ref):
        self.here, self.links = here, links
        self.shard_ref, self.full_ref = shard_ref, full_ref
        self.rows = shard_ref.shape[0]
        self.main = (self.rows - 2 * UNIT) // 8
        self.steps = range(1, lax.axis_size("dp"))
        self.slots = {}
        self.pending = []

    def slot(self, *key):
        if key not in self.slots:
            self.slots[key] = self.links.slot()
        return self.slots[key]

    def main_at(self, base, pos, first=0, count=None):
        start = base + (self.here.core * 4 + pos) * self.main + first
        return rows_of(self.full_ref, start, self.main if count is None else count)

    def extra_at(self, base):
        return rows_of(self.full_ref, base + 8 * self.main + self.here.core * UNIT, UNIT)

    def send(self, key, source, target, device, when=None):
        copy = self.links.copy(self.slot(*key), source, target, device)
        self.pending.append((copy, when))
        if when is None:
            copy.start()
        else:
            pl.when(when)(copy.start)

    def receive(self, key, target, when=None):
        copy = self.links.copy(self.slot(*key), target, target, self.here.plane(1))
        if when is None:
            copy.wait_recv()
        else:
            pl.when(when)(copy.wait_recv)

    def bases(self):
        for step in self.steps:
            shard = self.here.from_line(step)
            yield step, shard, shard * self.rows

    def start_line(self):
        here = self.here
        own = here.z * self.rows
        whole_shard = rows_of(self.full_ref, own, self.rows)
        self.send(("own",), self.shard_ref, whole_shard, here.plane(1))
        mine = here.pos == here.z % 4
        offset = (here.core * 4 + here.pos) * self.main
        for step in self.steps:
            device = here.line(step)
            source = rows_of(self.shard_ref, offset, self.main)
            self.send(("z", step), source, self.main_at(own, here.pos), device)
            source = rows_of(self.shard_ref, 8 * self.main + here.core * UNIT, UNIT)
            self.send(("ze", step), source, self.extra_at(own), device, mine)

    def wait_line(self):
        self.receive(("own",), rows_of(self.full_ref, self.here.z * self.rows, self.rows))
        for step, shard, base in self.bases():
            self.receive(("z", step), self.main_at(base, self.here.pos))
            self.receive(("ze", step), self.extra_at(base), self.here.pos == shard % 4)

    def start_sides(self, bases=None):
        here = self.here
        for step, shard, base in bases or self.bases():
            mine = here.pos == shard % 4
            for flip in (2, 4):
                piece = self.main_at(base, here.pos)
                self.send(("s", step, flip), piece, piece, here.plane(flip))
                piece = self.extra_at(base)
                self.send(("se", step, flip), piece, piece, here.plane(flip), mine)

    def wait_sides(self, bases=None):
        here = self.here
        for step, shard, base in bases or self.bases():
            for flip in (2, 4):
                pos = here.pos_near(flip)
                self.receive(("s", step, flip), self.main_at(base, pos))
                self.receive(("se", step, flip), self.extra_at(base), pos == shard % 4)

    def start_corner(self, bases=None):
        here = self.here
        half = self.main // 2
        for step, shard, base in bases or self.bases():
            piece = self.main_at(base, here.pos_near(2), 0, half)
            self.send(("d", step, 4), piece, piece, here.plane(4))
            piece = self.main_at(base, here.pos_near(4), half, half)
            self.send(("d", step, 2), piece, piece, here.plane(2))
            piece = self.extra_at(base)
            self.send(("de", step), piece, piece, here.plane(4), here.pos_near(2) == shard % 4)

    def wait_corner(self, bases=None):
        here = self.here
        half = self.main // 2
        for step, shard, base in bases or self.bases():
            pos = here.pos_near(6)
            self.receive(("d", step, 4), self.main_at(base, pos, 0, half))
            self.receive(("d", step, 2), self.main_at(base, pos, half, half))
            self.receive(("de", step), self.extra_at(base), pos == shard % 4)

    def core_part(self, base, core):
        main = rows_of(self.full_ref, base + core * 4 * self.main, 4 * self.main)
        return main, rows_of(self.full_ref, base + 8 * self.main + core * UNIT, UNIT)

    def start_core(self, bases=None):
        here = self.here
        for step, _, base in bases or self.bases():
            main, extra = self.core_part(base, here.core)
            self.send(("c", step), main, main, here.plane(1))
            self.send(("ce", step), extra, extra, here.plane(1))

    def wait_core(self, bases=None):
        for step, _, base in bases or self.bases():
            main, extra = self.core_part(base, 1 - self.here.core)
            self.receive(("c", step), main)
            self.receive(("ce", step), extra)

    def finish(self):
        for copy, when in self.pending:
            if when is None:
                copy.wait_send()
            else:
                pl.when(when)(copy.wait_send)
        self.pending = []

    def stages(self):
        def last():
            self.wait_core()
            self.finish()

        return [
            self.start_line,
            lambda: (self.wait_line(), self.start_sides()),
            lambda: (self.wait_sides(), self.start_corner()),
            lambda: (self.wait_corner(), self.start_core()),
            last,
        ]


class Swap:
    def __init__(self, here, links, source_ref, target_ref, local_sem):
        self.here, self.links = here, links
        self.source_ref, self.target_ref, self.local_sem = source_ref, target_ref, local_sem
        self.slots = {flip: links.slot() for flip in range(1, 8)}

    def copies(self):
        here = self.here
        for flip in (6, 2, 4, 7, 3, 5, 1):
            other = here.near(flip)
            out = self.links.copy(
                self.slots[flip],
                self.source_ref.at[other],
                self.target_ref.at[here.j],
                here.plane(flip),
            )
            back = self.links.copy(
                self.slots[flip],
                self.source_ref.at[other],
                self.target_ref.at[other],
                here.plane(flip),
            )
            yield out, back

    def start(self):
        here = self.here
        for out, _ in self.copies():
            out.start()
        self.local = pltpu.make_async_copy(
            self.source_ref.at[here.j], self.target_ref.at[here.j], self.local_sem
        )
        self.local.start()

    def wait(self):
        for out, back in self.copies():
            out.wait_send()
            back.wait_recv()
        self.local.wait()


def partners(here):
    plane = [here.plane(flip) for flip in range(1, 8)]
    return plane + [here.line(step) for step in range(1, lax.axis_size("dp"))]


def gather_small(here, links, small_ref, all_ref):
    all_ref[here.z] = small_ref[...]
    copies = []
    for step in range(1, lax.axis_size("dp")):
        slot = links.slot()
        copy = links.copy(slot, small_ref, all_ref.at[here.z], here.line(step))
        copy.start()
        copies.append((copy, links.copy(slot, small_ref, all_ref.at[here.from_line(step)], here.line(step))))
    return copies


def open_kernel(weights, *refs):
    shards = refs[:weights]
    tokens_ref, cot_ref, small_ref = refs[weights : weights + 3]
    fulls = refs[weights + 3 : 2 * weights + 3]
    image_ref, upstream_ref, all_ref, send_ref, recv_ref, local_ref = refs[2 * weights + 3 :]
    here = Place()
    greet(partners(here))
    links = Links(send_ref, recv_ref)
    small = gather_small(here, links, small_ref, all_ref)
    first = Swap(here, links, tokens_ref, image_ref, local_ref.at[0])
    second = Swap(here, links, cot_ref, upstream_ref, local_ref.at[1])
    gathers = [
        Gather(here, links, shard, full).stages()
        for shard, full in zip(shards, fulls)
    ]
    first.start()
    for turn in range(weights + 4):
        for m, stages in enumerate(gathers):
            if 0 <= turn - m < 5:
                stages[turn - m]()
        if turn == 2:
            first.wait()
            second.start()
    second.wait()
    for copy, back in small:
        copy.wait_send()
        back.wait_recv()


def open_all(tokens, cot, small, shards):
    depth = lax.axis_size("dp")
    parts, slice_len, width = tokens.shape
    anywhere = pl.BlockSpec(memory_space=pl.ANY)
    vmem = pl.BlockSpec(memory_space=pltpu.VMEM)
    weights = len(shards)
    copies = 13 + depth + weights * (1 + 11 * (depth - 1))
    return pl.pallas_call(
        functools.partial(open_kernel, weights),
        in_specs=[anywhere] * (weights + 2) + [vmem],
        out_specs=[anywhere] * (weights + 2) + [vmem],
        out_shape=[
            jax.ShapeDtypeStruct((shard.shape[0] * depth, shard.shape[1]), shard.dtype)
            for shard in shards
        ]
        + [jax.ShapeDtypeStruct(tokens.shape, tokens.dtype)] * 2
        + [jax.ShapeDtypeStruct((depth, *small.shape), small.dtype)],
        scratch_shapes=[
            pltpu.SemaphoreType.DMA((copies,)),
            pltpu.SemaphoreType.DMA((copies,)),
            pltpu.SemaphoreType.DMA((2,)),
        ],
        compiler_params=pltpu.CompilerParams(collective_id=0, has_side_effects=True),
        name="open_all",
    )(*shards, tokens, cot, small)


def add_rows(target_ref, at, terms):
    total = terms[0].astype(F32)
    for term in terms[1:]:
        total += term.astype(F32)
    target_ref[pl.ds(at, UNIT), :] = total.astype(target_ref.dtype)


class Reduce:
    def __init__(self, here, links, grad_ref, result_ref, buffers):
        self.here, self.links = here, links
        self.grad_ref, self.result_ref = grad_ref, result_ref
        self.sum_ref, self.side_ref, self.next_ref, self.line_ref, self.own_ref, self.own_sem = buffers
        self.depth, self.half, self.columns = self.sum_ref.shape
        self.main = (self.half - UNIT) // 4
        self.rows = 2 * self.half
        self.slots = {}
        self.pending = []
        self.spread = Gather(here, links, result_ref, result_ref)

    def send(self, key, source, target, device, when=None):
        if key not in self.slots:
            self.slots[key] = self.links.slot()
        copy = self.links.copy(self.slots[key], source, target, device)
        self.pending.append((copy, when))
        if when is None:
            copy.start()
        else:
            pl.when(when)(copy.start)

    def receive(self, key, target, when=None):
        copy = self.links.copy(self.slots[key], target, target, self.here.plane(1))
        if when is None:
            copy.wait_recv()
        else:
            pl.when(when)(copy.wait_recv)

    def part(self, ref, shard, start, count):
        return ref.at[shard, pl.ds(pl.multiple_of(start, UNIT), count), :]

    def extra(self, ref, shard):
        start = ref.shape[1] - UNIT
        return ref.at[shard, pl.ds(start, UNIT), :]

    def accumulate(self, shard, start, ref, other, first, count):
        def step(i, carry):
            at = pl.ds(pl.multiple_of(start + i * UNIT, UNIT), UNIT)
            more = ref[other, pl.ds(pl.multiple_of(first + i * UNIT, UNIT), UNIT), :]
            total = self.sum_ref[shard, at, :].astype(F32) + more.astype(F32)
            self.sum_ref[shard, at, :] = total.astype(BF16)
            return carry

        lax.fori_loop(0, count // UNIT, step, 0)

    def start_pair(self):
        core = 1 - self.here.core
        for shard in range(self.depth):
            base = shard * self.rows
            source = rows_of(self.grad_ref, base + core * 4 * self.main, 4 * self.main)
            target = self.part(self.sum_ref, shard, 0, 4 * self.main)
            self.send(("c", shard), source, target, self.here.plane(1))
            source = rows_of(self.grad_ref, base + 8 * self.main + core * UNIT, UNIT)
            self.send(("ce", shard), source, self.extra(self.sum_ref, shard), self.here.plane(1))

    def wait_pair(self):
        for shard in range(self.depth):
            self.receive(("c", shard), self.part(self.sum_ref, shard, 0, 4 * self.main))
            self.receive(("ce", shard), self.extra(self.sum_ref, shard))
        core = self.here.core
        many = 4 * self.main // UNIT
        blocks = many + 1
        units = self.rows // UNIT

        def place(shard, i):
            last = i // many
            return shard * units + (1 - last) * (core * many + i) + last * (2 * many + core), 0

        def body(own_ref):
            shard, i = pl.program_id(0), pl.program_id(1)
            at = pl.ds(pl.multiple_of(i * UNIT, UNIT), UNIT)
            total = self.sum_ref[shard, at, :].astype(F32) + own_ref[...].astype(F32)
            self.sum_ref[shard, at, :] = total.astype(BF16)

        pltpu.emit_pipeline(
            body,
            grid=(self.depth, blocks),
            in_specs=[pl.BlockSpec((UNIT, self.columns), place)],
        )(self.grad_ref)

    def first_side(self, shard):
        here, owner = self.here, shard % 4
        x_off, y_off = here.x != owner % 2, here.y != owner // 2
        if shard < self.depth // 2:
            return 2, 4, x_off, y_off
        return 4, 2, y_off, x_off

    def start_sides(self):
        here, main = self.here, self.main
        for shard in range(self.depth):
            flip, _, off, _ = self.first_side(shard)
            device = here.plane(flip)
            if flip == 2:
                for y in range(2):
                    source = self.part(self.sum_ref, shard, (2 * y + 1 - here.x) * main, main)
                    target = self.part(self.side_ref, shard, y * main, main)
                    self.send(("s", shard, y), source, target, device)
            else:
                source = self.part(self.sum_ref, shard, (1 - here.y) * 2 * main, 2 * main)
                target = self.part(self.side_ref, shard, 0, 2 * main)
                self.send(("s", shard, 0), source, target, device)
            extra = self.extra(self.side_ref, shard)
            self.send(("se", shard), self.extra(self.sum_ref, shard), extra, device, off)

    def wait_sides(self):
        here, main = self.here, self.main
        for shard in range(self.depth):
            flip, _, off, _ = self.first_side(shard)
            if flip == 2:
                for y in range(2):
                    self.receive(("s", shard, y), self.part(self.side_ref, shard, y * main, main))
                    self.accumulate(
                        shard, (2 * y + here.x) * main, self.side_ref, shard, y * main, main
                    )
            else:
                self.receive(("s", shard, 0), self.part(self.side_ref, shard, 0, 2 * main))
                self.accumulate(shard, here.y * 2 * main, self.side_ref, shard, 0, 2 * main)

            def take(shard=shard):
                self.receive(("se", shard), self.extra(self.side_ref, shard))
                self.accumulate(shard, 4 * main, self.side_ref, shard, 2 * main, UNIT)

            pl.when(jnp.logical_not(off))(take)

    def start_next(self):
        here, main = self.here, self.main
        for shard in range(self.depth):
            _, flip, off, off_next = self.first_side(shard)
            device = here.plane(flip)
            source = self.part(self.sum_ref, shard, here.pos_near(flip) * main, main)
            target = self.part(self.next_ref, shard, 0, main)
            self.send(("n", shard), source, target, device)
            when = jnp.logical_and(jnp.logical_not(off), off_next)
            extra = self.extra(self.next_ref, shard)
            self.send(("ne", shard), self.extra(self.sum_ref, shard), extra, device, when)

    def wait_next(self):
        here, main = self.here, self.main
        for shard in range(self.depth):
            self.receive(("n", shard), self.part(self.next_ref, shard, 0, main))
            self.accumulate(shard, here.pos * main, self.next_ref, shard, 0, main)

            def take(shard=shard):
                self.receive(("ne", shard), self.extra(self.next_ref, shard))
                self.accumulate(shard, 4 * main, self.next_ref, shard, main, UNIT)

            pl.when(here.pos == shard % 4)(take)

    def start_line(self):
        here, main = self.here, self.main
        for step in range(1, self.depth):
            device = here.line(step)
            shard = device[0]
            source = self.part(self.sum_ref, shard, here.pos * main, main)
            self.send(("l", step), source, self.part(self.line_ref, step - 1, 0, main), device)
            extra = self.extra(self.line_ref, step - 1)
            when = here.pos == shard % 4
            self.send(("le", step), self.extra(self.sum_ref, shard), extra, device, when)

    def wait_line(self):
        here, main = self.here, self.main
        for step in range(1, self.depth):
            self.receive(("l", step), self.part(self.line_ref, step - 1, 0, main))

        def total(start, first, count):
            def step(i, carry):
                at = pl.ds(pl.multiple_of(first + i * UNIT, UNIT), UNIT)
                own = pl.ds(pl.multiple_of(start + i * UNIT, UNIT), UNIT)
                value = self.sum_ref[here.z, own, :].astype(F32)
                for other in range(self.depth - 1):
                    value += self.line_ref[other, at, :].astype(F32)
                self.own_ref[at, :] = value.astype(BF16)
                return carry

            lax.fori_loop(0, count // UNIT, step, 0)

        total(here.pos * main, 0, main)
        target = rows_of(self.result_ref, (here.core * 4 + here.pos) * main, main)
        copy = pltpu.make_async_copy(self.own_ref.at[pl.ds(0, main), :], target, self.own_sem.at[0])
        copy.start()

        def take():
            for step in range(1, self.depth):
                self.receive(("le", step), self.extra(self.line_ref, step - 1))
            total(4 * main, main, UNIT)
            target = rows_of(self.result_ref, 8 * main + here.core * UNIT, UNIT)
            extra = pltpu.make_async_copy(
                self.own_ref.at[pl.ds(main, UNIT), :], target, self.own_sem.at[1]
            )
            extra.start()
            extra.wait()

        pl.when(here.pos == here.z % 4)(take)
        copy.wait()

    def stages(self):
        spread = self.spread
        bases = [(0, self.here.z, 0)]

        def last():
            spread.wait_core(bases)
            spread.finish()
            for copy, when in self.pending:
                if when is None:
                    copy.wait_send()
                else:
                    pl.when(when)(copy.wait_send)

        return [
            self.start_pair,
            lambda: (self.wait_pair(), self.start_sides()),
            lambda: (self.wait_sides(), self.start_next()),
            lambda: (self.wait_next(), self.start_line()),
            lambda: (self.wait_line(), spread.start_sides(bases)),
            lambda: (spread.wait_sides(bases), spread.start_corner(bases)),
            lambda: (spread.wait_corner(bases), spread.start_core(bases)),
            last,
        ]

    @staticmethod
    def buffers(depth, rows, columns):
        half = rows // 2
        main = (half - UNIT) // 4
        return [
            pltpu.VMEM((depth, half, columns), BF16),
            pltpu.VMEM((depth, 2 * main + UNIT, columns), BF16),
            pltpu.VMEM((depth, main + UNIT, columns), BF16),
            pltpu.VMEM((depth - 1, main + UNIT, columns), BF16),
            pltpu.VMEM((main + UNIT, columns), BF16),
            pltpu.SemaphoreType.DMA((2,)),
        ]

    @staticmethod
    def copies(depth):
        return 2 * depth + 3 * depth + 2 * depth + 2 * (depth - 1) + 9


def sum_small(here, links, small_ref, line_ref, plane_ref, result_ref):
    depth = lax.axis_size("dp")
    copies = []
    for step in range(1, depth):
        device = here.line(step)
        copy = links.copy(links.slot(), small_ref.at[device[0]], line_ref.at[step - 1], device)
        copy.start()
        copies.append(copy)
    total = small_ref[here.z]
    for step, copy in enumerate(copies):
        copy.wait()
        total += line_ref[step]
    plane_ref[here.j] = total
    copies = []
    for flip in range(1, 8):
        slot = links.slot()
        own = plane_ref.at[here.j]
        copy = links.copy(slot, own, own, here.plane(flip))
        copy.start()
        other = plane_ref.at[here.near(flip)]
        copies.append((copy, links.copy(slot, other, other, here.plane(flip))))
    for copy, back in copies:
        copy.wait_send()
        back.wait_recv()
    total = plane_ref[0]
    for other in range(1, 8):
        total += plane_ref[other]
    result_ref[...] = total


def close_kernel(weights, *refs):
    grads = refs[:weights]
    small_ref, out_ref, back_ref = refs[weights : weights + 3]
    results = refs[weights + 3 : 2 * weights + 3]
    sum_ref, layer_ref, input_ref = refs[2 * weights + 3 : 2 * weights + 6]
    send_ref, recv_ref, local_ref, line_ref, plane_ref = refs[2 * weights + 6 : 2 * weights + 11]
    scratch = refs[2 * weights + 11 :]
    here = Place()
    greet(partners(here))
    links = Links(send_ref, recv_ref)
    first = Swap(here, links, out_ref, layer_ref, local_ref.at[0])
    second = Swap(here, links, back_ref, input_ref, local_ref.at[1])
    reduces = [
        Reduce(here, links, grad, result, scratch[6 * m : 6 * m + 6]).stages()
        for m, (grad, result) in enumerate(zip(grads, results))
    ]
    for turn in range(weights + 7):
        for m, stages in enumerate(reduces):
            if 0 <= turn - m < 8:
                stages[turn - m]()
        if turn == 0:
            first.start()
        if turn == 3:
            first.wait()
            second.start()
    second.wait()
    sum_small(here, links, small_ref, line_ref, plane_ref, sum_ref)


def close_all(grads, small, out, back):
    depth = lax.axis_size("dp")
    rows = grads[0].shape[0] // depth
    anywhere = pl.BlockSpec(memory_space=pl.ANY)
    vmem = pl.BlockSpec(memory_space=pltpu.VMEM)
    weights = len(grads)
    copies = 14 + 7 + depth - 1 + weights * Reduce.copies(depth)
    scratch = []
    for grad in grads:
        scratch += Reduce.buffers(depth, rows, grad.shape[1])
    return pl.pallas_call(
        functools.partial(close_kernel, weights),
        in_specs=[anywhere] * weights + [vmem, anywhere, anywhere],
        out_specs=[anywhere] * weights + [vmem, anywhere, anywhere],
        out_shape=[jax.ShapeDtypeStruct((rows, grad.shape[1]), grad.dtype) for grad in grads]
        + [jax.ShapeDtypeStruct(small.shape[1:], small.dtype)]
        + [jax.ShapeDtypeStruct(out.shape, out.dtype)] * 2,
        scratch_shapes=[
            pltpu.SemaphoreType.DMA((copies,)),
            pltpu.SemaphoreType.DMA((copies,)),
            pltpu.SemaphoreType.DMA((2,)),
            pltpu.VMEM((depth - 1, *small.shape[1:]), F32),
            pltpu.VMEM((8, *small.shape[1:]), F32),
        ]
        + scratch,
        compiler_params=pltpu.CompilerParams(
            collective_id=1, has_side_effects=True, vmem_limit_bytes=60 * 1024 * 1024
        ),
        name="close_all",
    )(*grads, small, out, back)


def shards_image(
    tokens,
    key_mask,
    cotangent,
    qkv_weight,
    output_weight,
    expand_weight,
    contract_weight,
    norm1_gain,
    norm1_bias,
    query_bias,
    value_bias,
    output_bias,
    norm2_gain,
    norm2_bias,
    expand_bias,
    contract_bias,
):
    images_here, slice_len, width = tokens.shape
    length = slice_len * lax.axis_size("seq")

    vectors = (
        norm1_gain,
        norm1_bias,
        query_bias,
        value_bias,
        output_bias,
        norm2_gain,
        norm2_bias,
        expand_bias,
        contract_bias,
    )
    depth = lax.axis_size("dp")
    sizes = [vector.shape[0] for vector in vectors]
    block = 16 * 128
    padded = -(-sum(sizes) // block) * block
    joined = jnp.pad(jnp.concatenate(vectors), (0, padded - sum(sizes))).reshape(-1, 128)
    qkv_full, output_full, expand_full, contract_full, image, upstream, joined = open_all(
        tokens, cotangent, joined, (qkv_weight, output_weight, expand_weight, contract_weight)
    )
    image = image.reshape(length, width)
    upstream = upstream.reshape(length, width)
    joined = joined.reshape(depth, padded)
    full = []
    start = 0
    for size in sizes:
        full.append(joined[:, start : start + size].reshape(1, -1).astype(F32))
        start += size
    gain_one, shift_one, bias_q, bias_v, bias_out, gain_two, shift_two, bias_up, bias_down = full
    bias_three = jnp.concatenate([bias_q, jnp.zeros_like(bias_q), bias_v], axis=1).reshape(-1, 1)

    mask_row = lax.dynamic_slice_in_dim(key_mask, lax.axis_index("seq"), 1, 0)
    masked = jnp.where(mask_row > 0, 0.0, NEGATIVE)
    mask_rows = jnp.concatenate([masked, jnp.zeros((7, length), F32)], axis=0)

    packed, normed_t = qkv_forward(image, gain_one, shift_one, qkv_full, bias_three)
    raised, context_t, inverse = attend_forward(packed, mask_rows)
    middle, normed_two = join_forward(
        image, context_t, output_full, bias_out, gain_two, shift_two
    )
    out, middle_grad, expand_grad, contract_grad, up_grad, sums_two = mlp_both(
        normed_two, upstream, expand_full, contract_full, bias_up, middle, bias_down, gain_two
    )
    context_grad, output_grad = branch_back(middle_grad, context_t, output_full)
    packed_grad = attend_back(packed, context_grad, context_t, inverse, raised)
    packed_grad = packed_grad.reshape(3 * width, length)
    input_grad, qkv_grad, bias_grad, sums_one = input_back(
        normed_t, packed_grad, qkv_full, image, middle_grad, gain_one
    )

    bias_grad = bias_grad.reshape(3, width)
    small = (
        sums_one[0],
        sums_one[1],
        bias_grad[0],
        bias_grad[2],
        sums_two[2],
        sums_two[0],
        sums_two[1],
        up_grad[0],
        sums_two[3],
    )
    small = jnp.concatenate([part.reshape(depth, -1) for part in small], axis=1)
    small = jnp.pad(small, ((0, 0), (0, padded - sum(sizes)))).reshape(depth, -1, 128)
    *weight_grads, small, out, input_grad = close_all(
        (qkv_grad, output_grad, expand_grad, contract_grad),
        small,
        out.reshape(images_here, slice_len, width),
        input_grad.reshape(images_here, slice_len, width),
    )
    small = small.reshape(-1)
    outs = []
    start = 0
    for size in sizes:
        outs.append(small[start : start + size])
        start += size
    return (out, input_grad, *[grad.astype(F32) for grad in weight_grads], *outs)


def solution(mesh):
    def apply(*arguments):
        images_here = arguments[0].shape[0] // mesh.shape["dp"]
        whole_images = images_here == mesh.shape["seq"]
        body = shards_image if whole_images else shards_general
        return jax.shard_map(
            body, mesh=mesh, in_specs=in_specs, out_specs=out_specs, check_vma=False
        )(*arguments)

    in_specs = (
        P("dp", "seq", None),
        P("dp", None),
        P("dp", "seq", None),
        P("dp", None),
        P("dp", None),
        P("dp", None),
        P("dp", None),
        P("dp"),
        P("dp"),
        P("dp"),
        P("dp"),
        P("dp"),
        P("dp"),
        P("dp"),
        P("dp"),
        P("dp"),
    )
    out_specs = (
        P("dp", "seq", None),
        P("dp", "seq", None),
        P("dp", None),
        P("dp", None),
        P("dp", None),
        P("dp", None),
        P("dp"),
        P("dp"),
        P("dp"),
        P("dp"),
        P("dp"),
        P("dp"),
        P("dp"),
        P("dp"),
        P("dp"),
    )
    return apply
```

```python
import functools

import jax
import jax.numpy as jnp
from jax import lax
from jax.experimental import pallas as pl
from jax.experimental.pallas import tpu as pltpu
from jax.sharding import PartitionSpec as P

HEAD_DIM = 72


EPSILON = 1e-06
GELU_COEF = 0.7978845608028654
NEGATIVE = -1000000000.0


def layer_norm(values, scale_gain, shift_bias):
    center = values - jnp.mean(values, axis=-1, keepdims=True)
    spread = jnp.mean(center * center, axis=-1, keepdims=True)
    return center * lax.rsqrt(spread + EPSILON) * scale_gain + shift_bias


def gelu_tanh(values):
    return (
        0.5 * values * (1.0 + jnp.tanh(GELU_COEF * (values + 0.044715 * values * values * values)))
    )


def attend_scores(query_heads, key_heads, key_valid):
    raw_scores = jnp.einsum(
        "bqhd,bkhd->bhqk", query_heads, key_heads, preferred_element_type=jnp.float32
    )
    raw_scores = raw_scores * HEAD_DIM ** (-0.5)
    return jnp.where(key_valid[:, None, None, :], raw_scores, NEGATIVE)


def shards_general(
    tokens,
    key_mask,
    cotangent,
    qkv_weight,
    output_weight,
    expand_weight,
    contract_weight,
    norm1_gain,
    norm1_bias,
    query_bias,
    value_bias,
    output_bias,
    norm2_gain,
    norm2_bias,
    expand_bias,
    contract_bias,
):
    images_here, slice_len, feature_width = tokens.shape
    seq_count = lax.axis_size("seq")
    total_rows = images_here * slice_len
    full_length = slice_len * seq_count
    local_width = feature_width // seq_count
    local_heads = local_width // HEAD_DIM
    row_dims = (((0,), (0,)), ((), ()))
    col_dims = (((1,), (1,)), ((), ()))
    (
        qkv_full,
        output_full,
        expand_full,
        contract_full,
        gain_one,
        shift_one,
        query_shift,
        value_shift,
        output_shift,
        gain_two,
        shift_two,
        expand_shift,
        contract_shift,
    ) = (
        lax.all_gather(qkv_weight, "dp", axis=0, tiled=True),
        lax.all_gather(output_weight, "dp", axis=0, tiled=True),
        lax.all_gather(expand_weight, "dp", axis=0, tiled=True),
        lax.all_gather(contract_weight, "dp", axis=0, tiled=True),
        lax.all_gather(norm1_gain, "dp", axis=0, tiled=True),
        lax.all_gather(norm1_bias, "dp", axis=0, tiled=True),
        lax.all_gather(query_bias, "dp", axis=0, tiled=True),
        lax.all_gather(value_bias, "dp", axis=0, tiled=True),
        lax.all_gather(output_bias, "dp", axis=0, tiled=True),
        lax.all_gather(norm2_gain, "dp", axis=0, tiled=True),
        lax.all_gather(norm2_bias, "dp", axis=0, tiled=True),
        lax.all_gather(expand_bias, "dp", axis=0, tiled=True),
        lax.all_gather(contract_bias, "dp", axis=0, tiled=True),
    )
    inputs = tokens.reshape(total_rows, feature_width).astype(jnp.float32)
    normed, norm_one_back = jax.vjp(
        layer_norm, inputs, gain_one.astype(jnp.float32), shift_one.astype(jnp.float32)
    )
    normed_low = normed.astype(jnp.bfloat16)
    bias_three = jnp.concatenate([query_shift, jnp.zeros_like(query_shift), value_shift]).astype(
        jnp.float32
    )
    packed = jnp.dot(normed_low, qkv_full, preferred_element_type=jnp.float32) + bias_three
    packed = packed.astype(jnp.bfloat16).reshape(images_here, slice_len, 3, feature_width)
    by_heads = lax.all_to_all(packed, "seq", split_axis=3, concat_axis=1, tiled=True)
    head_shape = (images_here, full_length, local_heads, HEAD_DIM)
    query_heads = by_heads[:, :, 0].reshape(head_shape)
    key_heads = by_heads[:, :, 1].reshape(head_shape)
    value_heads = by_heads[:, :, 2].reshape(head_shape)
    key_valid = key_mask > 0
    scores = attend_scores(query_heads, key_heads, key_valid)
    row_peak = jnp.max(scores, axis=-1, keepdims=True)
    raised = jnp.exp(scores - row_peak)
    totals = jnp.sum(raised, axis=-1, keepdims=True)
    soft_probs = raised / totals
    log_total = row_peak + jnp.log(totals)
    probs_low = soft_probs.astype(jnp.bfloat16)
    context = jnp.einsum(
        "bhqk,bkhd->bqhd", probs_low, value_heads, preferred_element_type=jnp.float32
    )
    context = context.reshape(images_here, full_length, local_width).astype(jnp.bfloat16)
    by_tokens = lax.all_to_all(context, "seq", split_axis=1, concat_axis=2, tiled=True)
    context_rows = by_tokens.reshape(total_rows, feature_width)
    branch = jnp.dot(
        context_rows, output_full, preferred_element_type=jnp.float32
    ) + output_shift.astype(jnp.float32)
    middle = inputs + branch
    normed_two, norm_two_back = jax.vjp(
        layer_norm, middle, gain_two.astype(jnp.float32), shift_two.astype(jnp.float32)
    )
    normed_two_low = normed_two.astype(jnp.bfloat16)
    hidden_pre = jnp.dot(
        normed_two_low, expand_full, preferred_element_type=jnp.float32
    ) + expand_shift.astype(jnp.float32)
    activated, gelu_back = jax.vjp(gelu_tanh, hidden_pre)
    activated_low = activated.astype(jnp.bfloat16)
    mlp_out = lax.dot_general(
        activated_low, contract_full, col_dims, preferred_element_type=jnp.float32
    )
    mlp_out = mlp_out + contract_shift.astype(jnp.float32)
    layer_out = (middle + mlp_out).astype(jnp.bfloat16).reshape(tokens.shape)
    qkv_back, output_back, expand_back, contract_back = (
        lax.all_gather(qkv_weight, "dp", axis=0, tiled=True),
        lax.all_gather(output_weight, "dp", axis=0, tiled=True),
        lax.all_gather(expand_weight, "dp", axis=0, tiled=True),
        lax.all_gather(contract_weight, "dp", axis=0, tiled=True),
    )
    upstream = cotangent.reshape(total_rows, feature_width).astype(jnp.float32)
    mlp_grad = cotangent.reshape(total_rows, feature_width)
    grad_contract_bias = jnp.sum(upstream, axis=0)
    grad_contract = lax.dot_general(
        mlp_grad, activated_low, row_dims, preferred_element_type=jnp.float32
    )
    act_grad = jnp.dot(mlp_grad, contract_back, preferred_element_type=jnp.float32)
    (pre_grad,) = gelu_back(act_grad)
    pre_low = pre_grad.astype(jnp.bfloat16)
    grad_expand_bias = jnp.sum(pre_low.astype(jnp.float32), axis=0)
    grad_expand = lax.dot_general(
        normed_two_low, pre_low, row_dims, preferred_element_type=jnp.float32
    )
    normed_two_grad = lax.dot_general(
        pre_low, expand_back, col_dims, preferred_element_type=jnp.float32
    )
    middle_part, grad_gain_two, grad_shift_two = norm_two_back(normed_two_grad)
    middle_grad = upstream + middle_part
    branch_low = middle_grad.astype(jnp.bfloat16)
    grad_output_bias = jnp.sum(branch_low.astype(jnp.float32), axis=0)
    grad_output = lax.dot_general(
        context_rows, branch_low, row_dims, preferred_element_type=jnp.float32
    )
    context_grad = lax.dot_general(
        branch_low, output_back, col_dims, preferred_element_type=jnp.float32
    )
    context_grad = context_grad.astype(jnp.bfloat16).reshape(images_here, slice_len, feature_width)
    grad_heads = lax.all_to_all(
        context_grad, "seq", split_axis=2, concat_axis=1, tiled=True
    ).reshape(head_shape)
    scores_again = attend_scores(query_heads, key_heads, key_valid)
    probs_again = jnp.exp(scores_again - log_total)
    probs_again_low = probs_again.astype(jnp.bfloat16)
    prob_grad = jnp.einsum(
        "bqhd,bkhd->bhqk", grad_heads, value_heads, preferred_element_type=jnp.float32
    )
    value_grad = jnp.einsum(
        "bhqk,bqhd->bkhd", probs_again_low, grad_heads, preferred_element_type=jnp.float32
    )
    row_dot = jnp.sum(probs_again * prob_grad, axis=-1, keepdims=True)
    score_low = (probs_again * (prob_grad - row_dot)).astype(jnp.bfloat16)
    query_grad = jnp.einsum(
        "bhqk,bkhd->bqhd", score_low, key_heads, preferred_element_type=jnp.float32
    ) * HEAD_DIM ** (-0.5)
    key_grad = jnp.einsum(
        "bhqk,bqhd->bkhd", score_low, query_heads, preferred_element_type=jnp.float32
    ) * HEAD_DIM ** (-0.5)
    stacked = jnp.stack([query_grad, key_grad, value_grad], axis=2)
    stacked = stacked.reshape(images_here, full_length, 3, local_width).astype(jnp.bfloat16)
    back_packed = lax.all_to_all(stacked, "seq", split_axis=1, concat_axis=3, tiled=True)
    packed_grad = back_packed.reshape(total_rows, 3 * feature_width)
    grad_query_bias = jnp.sum(packed_grad[:, :feature_width].astype(jnp.float32), axis=0)
    grad_value_bias = jnp.sum(packed_grad[:, 2 * feature_width :].astype(jnp.float32), axis=0)
    grad_qkv = lax.dot_general(
        normed_low, packed_grad, row_dims, preferred_element_type=jnp.float32
    )
    normed_grad = lax.dot_general(
        packed_grad, qkv_back, col_dims, preferred_element_type=jnp.float32
    )
    input_part, grad_gain_one, grad_shift_one = norm_one_back(normed_grad)
    input_grad = (middle_grad + input_part).astype(jnp.bfloat16).reshape(tokens.shape)
    shares = (
        lax.psum_scatter(grad_qkv, ("dp", "seq"), scatter_dimension=0, tiled=True),
        lax.psum_scatter(grad_output, ("dp", "seq"), scatter_dimension=0, tiled=True),
        lax.psum_scatter(grad_expand, ("dp", "seq"), scatter_dimension=0, tiled=True),
        lax.psum_scatter(grad_contract, ("dp", "seq"), scatter_dimension=0, tiled=True),
        lax.psum_scatter(grad_gain_one, ("dp", "seq"), scatter_dimension=0, tiled=True),
        lax.psum_scatter(grad_shift_one, ("dp", "seq"), scatter_dimension=0, tiled=True),
        lax.psum_scatter(grad_query_bias, ("dp", "seq"), scatter_dimension=0, tiled=True),
        lax.psum_scatter(grad_value_bias, ("dp", "seq"), scatter_dimension=0, tiled=True),
        lax.psum_scatter(grad_output_bias, ("dp", "seq"), scatter_dimension=0, tiled=True),
        lax.psum_scatter(grad_gain_two, ("dp", "seq"), scatter_dimension=0, tiled=True),
        lax.psum_scatter(grad_shift_two, ("dp", "seq"), scatter_dimension=0, tiled=True),
        lax.psum_scatter(grad_contract_bias, ("dp", "seq"), scatter_dimension=0, tiled=True),
    )
    summed = (
        lax.all_gather(shares[0].astype(jnp.bfloat16), "seq", axis=0, tiled=True).astype(
            jnp.float32
        ),
        lax.all_gather(shares[1].astype(jnp.bfloat16), "seq", axis=0, tiled=True).astype(
            jnp.float32
        ),
        lax.all_gather(shares[2].astype(jnp.bfloat16), "seq", axis=0, tiled=True).astype(
            jnp.float32
        ),
        lax.all_gather(shares[3].astype(jnp.bfloat16), "seq", axis=0, tiled=True).astype(
            jnp.float32
        ),
        lax.all_gather(shares[4].astype(jnp.bfloat16), "seq", axis=0, tiled=True).astype(
            jnp.float32
        ),
        lax.all_gather(shares[5].astype(jnp.bfloat16), "seq", axis=0, tiled=True).astype(
            jnp.float32
        ),
        lax.all_gather(shares[6].astype(jnp.bfloat16), "seq", axis=0, tiled=True).astype(
            jnp.float32
        ),
        lax.all_gather(shares[7].astype(jnp.bfloat16), "seq", axis=0, tiled=True).astype(
            jnp.float32
        ),
        lax.all_gather(shares[8].astype(jnp.bfloat16), "seq", axis=0, tiled=True).astype(
            jnp.float32
        ),
        lax.all_gather(shares[9].astype(jnp.bfloat16), "seq", axis=0, tiled=True).astype(
            jnp.float32
        ),
        lax.all_gather(shares[10].astype(jnp.bfloat16), "seq", axis=0, tiled=True).astype(
            jnp.float32
        ),
        lax.all_gather(shares[11].astype(jnp.bfloat16), "seq", axis=0, tiled=True).astype(
            jnp.float32
        ),
    )
    hidden_total = lax.psum(grad_expand_bias, ("dp", "seq"))
    share_rows = hidden_total.shape[0] // lax.axis_size("dp")
    expand_bias_part = lax.dynamic_slice_in_dim(
        hidden_total, lax.axis_index("dp") * share_rows, share_rows, 0
    )
    final = tuple(summed) + (expand_bias_part,)
    return (
        layer_out,
        input_grad,
        final[0],
        final[1],
        final[2],
        final[3],
        final[4],
        final[5],
        final[6],
        final[7],
        final[8],
        final[9],
        final[10],
        final[12],
        final[11],
    )


F32 = jnp.float32
BF16 = jnp.bfloat16
SCALE = HEAD_DIM ** (-0.5)
LOG2_E = 1.4426950408889634
MIB = 1024 * 1024
UNIT = 16
MESH_ID = pl.DeviceIdType.MESH
NN = (((1,), (0,)), ((), ()))
NT = (((1,), (1,)), ((), ()))
TN = (((0,), (0,)), ((), ()))
ANY = pl.BlockSpec(memory_space=pl.ANY)
SEMAPHORES = 160


def mm(left, right, dims):
    return lax.dot_general(left, right, dims, preferred_element_type=F32)


def whole(shape):
    return pl.BlockSpec(shape, lambda *_: (0,) * len(shape), pipeline_mode=pl.Buffered(1))


def shape_of(dims, dtype):
    return jax.ShapeDtypeStruct(dims, dtype)


def centred(values):
    center = values - jnp.mean(values, axis=-1, keepdims=True)
    rate = lax.rsqrt(jnp.mean(center * center, axis=-1, keepdims=True) + EPSILON)
    return center * rate, rate


class Place:
    def __init__(self):
        self.depth = lax.axis_size("dp")
        self.z = lax.axis_index("dp")
        self.j = lax.axis_index("seq")
        self.core = self.j % 2
        self.x = (self.j // 2) % 2
        self.y = self.j // 4
        self.pos = self.j // 2

    def near(self, flip):
        other = self.j
        if flip & 1:
            other = other + 1 - 2 * self.core
        if flip & 2:
            other = other + 2 - 4 * self.x
        if flip & 4:
            other = other + 4 - 8 * self.y
        return other

    def plane(self, flip):
        return (self.z, self.near(flip))

    def pos_near(self, flip):
        return self.near(flip) // 2

    def line(self, step):
        return ((self.z + step) % self.depth, self.j)

    def from_line(self, step):
        return (self.z + self.depth - step) % self.depth

    def greet(self, flips, line):
        devices = [self.plane(flip) for flip in flips]
        if line:
            devices += [self.line(step) for step in range(1, self.depth)]
        barrier = pltpu.get_barrier_semaphore()
        for device in devices:
            pl.semaphore_signal(barrier, inc=1, device_id=device, device_id_type=MESH_ID)
        pl.semaphore_wait(barrier, len(devices))


class Links:
    def __init__(self, send_ref, recv_ref):
        self.send_ref, self.recv_ref, self.used = send_ref, recv_ref, 0

    def slot(self):
        self.used += 1
        return self.used - 1

    def copy(self, slot, source, target, device):
        return pltpu.make_async_remote_copy(
            src_ref=source,
            dst_ref=target,
            send_sem=self.send_ref.at[slot],
            recv_sem=self.recv_ref.at[slot],
            device_id=device,
            device_id_type=MESH_ID,
        )


def at_step(step, *actions):
    @pl.when(pl.program_id(0) == step)
    def _():
        for action in actions:
            action()


def rows_of(ref, start, count):
    return ref.at[pl.ds(pl.multiple_of(start, UNIT), count), :]


class Wire:
    def __init__(self, here, links):
        self.here, self.links = here, links
        self.slots, self.begun, self.closing = {}, [], False

    def slot(self, key):
        if key not in self.slots:
            self.slots[key] = self.links.slot()
        return self.slots[key]

    def send(self, key, source, target, device, when=None):
        copy = self.links.copy(self.slot(key), source, target, device)
        act = copy.wait_send if self.closing else copy.start
        if when is None:
            act()
        else:
            pl.when(when)(act)

    def receive(self, key, target, when=None):
        copy = self.links.copy(self.slot(key), target, target, self.here.plane(1))
        if when is None:
            copy.wait_recv()
        else:
            pl.when(when)(copy.wait_recv)

    def begin(self, stage):
        self.begun.append(stage)
        stage()

    def finish(self):
        self.closing = True
        for stage in self.begun:
            stage()
        self.closing, self.begun = False, []


class Gather(Wire):
    def __init__(self, here, links, shard_ref, full_ref, own_only=False):
        super().__init__(here, links)
        self.shard_ref, self.full_ref = shard_ref, full_ref
        self.own_only = own_only
        self.rows = full_ref.shape[0] // (1 if own_only else here.depth)
        self.main = (self.rows - 2 * UNIT) // 8

    def bases(self):
        if self.own_only:
            yield 0, self.here.z, 0
            return
        for step in range(1, self.here.depth):
            shard = self.here.from_line(step)
            yield step, shard, shard * self.rows

    def main_at(self, base, pos, first=0, count=None):
        start = base + (self.here.core * 4 + pos) * self.main + first
        return rows_of(self.full_ref, start, self.main if count is None else count)

    def extra_at(self, base):
        return rows_of(self.full_ref, base + 8 * self.main + self.here.core * UNIT, UNIT)

    def start_line(self):
        here = self.here
        own = here.z * self.rows
        mine = here.pos == here.z % 4
        offset = (here.core * 4 + here.pos) * self.main
        for step in range(1, here.depth):
            device = here.line(step)
            source = rows_of(self.shard_ref, offset, self.main)
            self.send(("z", step), source, self.main_at(own, here.pos), device)
            source = rows_of(self.shard_ref, 8 * self.main + here.core * UNIT, UNIT)
            self.send(("ze", step), source, self.extra_at(own), device, mine)
        whole_shard = rows_of(self.full_ref, own, self.rows)
        self.send("own", self.shard_ref, whole_shard, here.plane(1))

    def wait_line(self):
        here = self.here
        for step, shard, base in self.bases():
            self.receive(("z", step), self.main_at(base, here.pos))
            self.receive(("ze", step), self.extra_at(base), here.pos == shard % 4)
        self.receive("own", rows_of(self.full_ref, here.z * self.rows, self.rows))

    def start_sides(self):
        here = self.here
        for step, shard, base in self.bases():
            mine = here.pos == shard % 4
            for flip in (2, 4):
                piece = self.main_at(base, here.pos)
                self.send(("s", step, flip), piece, piece, here.plane(flip))
                piece = self.extra_at(base)
                self.send(("se", step, flip), piece, piece, here.plane(flip), mine)

    def wait_sides(self):
        here = self.here
        for step, shard, base in self.bases():
            for flip in (2, 4):
                pos = here.pos_near(flip)
                self.receive(("s", step, flip), self.main_at(base, pos))
                self.receive(("se", step, flip), self.extra_at(base), pos == shard % 4)

    def start_corner(self):
        here = self.here
        half = self.main // 2
        for step, shard, base in self.bases():
            piece = self.main_at(base, here.pos_near(2), 0, half)
            self.send(("d", step, 4), piece, piece, here.plane(4))
            piece = self.main_at(base, here.pos_near(4), half, half)
            self.send(("d", step, 2), piece, piece, here.plane(2))
            piece = self.extra_at(base)
            self.send(("de", step), piece, piece, here.plane(4), here.pos_near(2) == shard % 4)

    def wait_corner(self):
        here = self.here
        half = self.main // 2
        for step, shard, base in self.bases():
            pos = here.pos_near(6)
            self.receive(("d", step, 4), self.main_at(base, pos, 0, half))
            self.receive(("d", step, 2), self.main_at(base, pos, half, half))
            self.receive(("de", step), self.extra_at(base), pos == shard % 4)

    def core_part(self, base, core):
        main = rows_of(self.full_ref, base + core * 4 * self.main, 4 * self.main)
        return main, rows_of(self.full_ref, base + 8 * self.main + core * UNIT, UNIT)

    def start_core(self):
        here = self.here
        for step, _, base in self.bases():
            main, extra = self.core_part(base, here.core)
            self.send(("c", step), main, main, here.plane(1))
            self.send(("ce", step), extra, extra, here.plane(1))

    def wait_core(self):
        for step, _, base in self.bases():
            main, extra = self.core_part(base, 1 - self.here.core)
            self.receive(("c", step), main)
            self.receive(("ce", step), extra)

    def line(self):
        self.begin(self.start_line)

    def sides(self):
        self.begin(self.start_sides)

    def corner(self):
        self.wait_sides()
        self.begin(self.start_corner)

    def core(self):
        self.wait_corner()
        self.begin(self.start_core)

    def end(self):
        self.wait_core()
        self.finish()

    def end_line(self):
        self.wait_line()
        self.finish()


class Swap:
    def __init__(self, here, links, source_ref, target_ref, local_sem):
        self.here, self.links = here, links
        self.source_ref, self.target_ref, self.local_sem = source_ref, target_ref, local_sem
        self.slots = {flip: links.slot() for flip in range(1, 8)}

    def copy(self, flip, landing):
        here = self.here
        return self.links.copy(
            self.slots[flip],
            self.source_ref.at[here.near(flip)],
            self.target_ref.at[landing],
            here.plane(flip),
        )

    def local(self):
        own = self.here.j
        return pltpu.make_async_copy(
            self.source_ref.at[own], self.target_ref.at[own], self.local_sem
        )

    def start(self):
        for flip in (6, 2, 4, 7, 3, 5, 1):
            self.copy(flip, self.here.j).start()
        self.local().start()

    def wait(self):
        for flip in range(1, 8):
            self.copy(flip, self.here.near(flip)).wait()
        self.local().wait()


class Reduce(Wire):
    def __init__(self, here, links, buffers, local_ref, grad_ref=None, result_ref=None):
        super().__init__(here, links)
        self.grad_ref, self.result_ref, self.local_ref = grad_ref, result_ref, local_ref
        self.sum_ref, self.stage_ref, self.side_ref, self.next_ref, self.line_ref, self.own_ref = buffers
        self.depth, self.half, self.columns = self.sum_ref.shape
        self.main = (self.half - UNIT) // 4
        self.rows = 2 * self.half
        if result_ref is not None:
            self.spread = Gather(here, links, None, result_ref, own_only=True)

    def part(self, ref, shard, start, count):
        return ref.at[shard, pl.ds(pl.multiple_of(start, UNIT), count), :]

    def extra(self, ref, shard):
        return ref.at[shard, pl.ds(ref.shape[1] - UNIT, UNIT), :]

    def accumulate(self, shard, start, ref, first, count):
        def step(i, carry):
            at = pl.ds(pl.multiple_of(start + i * UNIT, UNIT), UNIT)
            more = ref[shard, pl.ds(pl.multiple_of(first + i * UNIT, UNIT), UNIT), :]
            total = self.sum_ref[shard, at, :].astype(F32) + more.astype(F32)
            self.sum_ref[shard, at, :] = total.astype(BF16)
            return carry

        lax.fori_loop(0, count // UNIT, step, 0)

    def start_pair(self):
        core = 1 - self.here.core
        for shard in range(self.depth):
            base = shard * self.rows
            source = rows_of(self.grad_ref, base + core * 4 * self.main, 4 * self.main)
            target = self.part(self.sum_ref, shard, 0, 4 * self.main)
            self.send(("c", shard), source, target, self.here.plane(1))
            source = rows_of(self.grad_ref, base + 8 * self.main + core * UNIT, UNIT)
            self.send(("ce", shard), source, self.extra(self.sum_ref, shard), self.here.plane(1))

    def own_copies(self, shard):
        slot, base, core = shard % 2, shard * self.rows, self.here.core
        main = rows_of(self.grad_ref, base + core * 4 * self.main, 4 * self.main)
        extra = rows_of(self.grad_ref, base + 8 * self.main + core * UNIT, UNIT)
        return (
            pltpu.make_async_copy(
                main, self.part(self.stage_ref, slot, 0, 4 * self.main), self.local_ref.at[2 * slot]
            ),
            pltpu.make_async_copy(
                extra, self.extra(self.stage_ref, slot), self.local_ref.at[2 * slot + 1]
            ),
        )

    def start_own(self, shard):
        for copy in self.own_copies(shard):
            copy.start()

    def wait_pair(self):
        for shard in range(self.depth):
            self.receive(("c", shard), self.part(self.sum_ref, shard, 0, 4 * self.main))
            self.receive(("ce", shard), self.extra(self.sum_ref, shard))
            for copy in self.own_copies(shard):
                copy.wait()

            def step(i, carry, shard=shard):
                at = pl.ds(pl.multiple_of(i * UNIT, UNIT), UNIT)
                total = self.sum_ref[shard, at, :].astype(F32)
                total += self.stage_ref[shard % 2, at, :].astype(F32)
                self.sum_ref[shard, at, :] = total.astype(BF16)
                return carry

            lax.fori_loop(0, self.half // UNIT, step, 0)
            if shard + 2 < self.depth:
                self.start_own(shard + 2)

    def first_side(self, shard):
        here, owner = self.here, shard % 4
        x_off, y_off = here.x != owner % 2, here.y != owner // 2
        if shard < self.depth // 2:
            return 2, 4, x_off, y_off
        return 4, 2, y_off, x_off

    def start_sides(self):
        here, main = self.here, self.main
        for shard in range(self.depth):
            flip, _, off, _ = self.first_side(shard)
            device = here.plane(flip)
            if flip == 2:
                for y in range(2):
                    source = self.part(self.sum_ref, shard, (2 * y + 1 - here.x) * main, main)
                    target = self.part(self.side_ref, shard, y * main, main)
                    self.send(("s", shard, y), source, target, device)
            else:
                source = self.part(self.sum_ref, shard, (1 - here.y) * 2 * main, 2 * main)
                target = self.part(self.side_ref, shard, 0, 2 * main)
                self.send(("s", shard, 0), source, target, device)
            extra = self.extra(self.side_ref, shard)
            self.send(("se", shard), self.extra(self.sum_ref, shard), extra, device, off)

    def wait_sides(self):
        here, main = self.here, self.main
        for shard in range(self.depth):
            flip, _, off, _ = self.first_side(shard)
            if flip == 2:
                for y in range(2):
                    self.receive(("s", shard, y), self.part(self.side_ref, shard, y * main, main))
                    self.accumulate(shard, (2 * y + here.x) * main, self.side_ref, y * main, main)
            else:
                self.receive(("s", shard, 0), self.part(self.side_ref, shard, 0, 2 * main))
                self.accumulate(shard, here.y * 2 * main, self.side_ref, 0, 2 * main)

            def take(shard=shard):
                self.receive(("se", shard), self.extra(self.side_ref, shard))
                self.accumulate(shard, 4 * main, self.side_ref, 2 * main, UNIT)

            pl.when(jnp.logical_not(off))(take)

    def start_next(self):
        here, main = self.here, self.main
        for shard in range(self.depth):
            _, flip, off, off_next = self.first_side(shard)
            device = here.plane(flip)
            source = self.part(self.sum_ref, shard, here.pos_near(flip) * main, main)
            target = self.part(self.next_ref, shard, 0, main)
            self.send(("n", shard), source, target, device)
            when = jnp.logical_and(jnp.logical_not(off), off_next)
            extra = self.extra(self.next_ref, shard)
            self.send(("ne", shard), self.extra(self.sum_ref, shard), extra, device, when)

    def wait_next(self):
        here, main = self.here, self.main
        for shard in range(self.depth):
            self.receive(("n", shard), self.part(self.next_ref, shard, 0, main))
            self.accumulate(shard, here.pos * main, self.next_ref, 0, main)

            def take(shard=shard):
                self.receive(("ne", shard), self.extra(self.next_ref, shard))
                self.accumulate(shard, 4 * main, self.next_ref, main, UNIT)

            pl.when(here.pos == shard % 4)(take)

    def start_line(self):
        here, main = self.here, self.main
        for step in range(1, self.depth):
            device = here.line(step)
            shard = device[0]
            source = self.part(self.sum_ref, shard, here.pos * main, main)
            self.send(("l", step), source, self.part(self.line_ref, step - 1, 0, main), device)
            extra = self.extra(self.line_ref, step - 1)
            when = here.pos == shard % 4
            self.send(("le", step), self.extra(self.sum_ref, shard), extra, device, when)

    def wait_line(self):
        here, main = self.here, self.main
        for step in range(1, self.depth):
            self.receive(("l", step), self.part(self.line_ref, step - 1, 0, main))

        def total(start, first, count):
            def step(i, carry):
                at = pl.ds(pl.multiple_of(first + i * UNIT, UNIT), UNIT)
                own = pl.ds(pl.multiple_of(start + i * UNIT, UNIT), UNIT)
                value = self.sum_ref[here.z, own, :].astype(F32)
                for other in range(self.depth - 1):
                    value += self.line_ref[other, at, :].astype(F32)
                self.own_ref[at, :] = value.astype(BF16)
                return carry

            lax.fori_loop(0, count // UNIT, step, 0)

        total(here.pos * main, 0, main)
        target = rows_of(self.result_ref, (here.core * 4 + here.pos) * main, main)
        copy = pltpu.make_async_copy(
            self.own_ref.at[pl.ds(0, main), :], target, self.local_ref.at[0]
        )
        copy.start()

        def take():
            for step in range(1, self.depth):
                self.receive(("le", step), self.extra(self.line_ref, step - 1))
            total(4 * main, main, UNIT)
            target = rows_of(self.result_ref, 8 * main + here.core * UNIT, UNIT)
            extra = pltpu.make_async_copy(
                self.own_ref.at[pl.ds(main, UNIT), :], target, self.local_ref.at[1]
            )
            extra.start()
            extra.wait()

        pl.when(here.pos == here.z % 4)(take)
        copy.wait()

    def pair(self):
        self.begin(self.start_pair)
        self.start_own(0)
        self.start_own(1)

    def sides(self):
        self.wait_pair()
        self.begin(self.start_sides)

    def after_sides(self):
        self.wait_sides()
        self.begin(self.start_next)

    def after_next(self):
        self.wait_next()
        self.begin(self.start_line)

    def after_line(self):
        self.wait_line()
        self.spread.sides()

    def corner(self):
        self.spread.corner()

    def core(self):
        self.spread.core()

    def end(self):
        self.spread.end()
        self.finish()

    def save(self, state_ref):
        copy = pltpu.make_async_copy(self.sum_ref, state_ref, self.local_ref.at[0])
        copy.start()
        copy.wait()

    def load(self, state_ref):
        copy = pltpu.make_async_copy(state_ref, self.sum_ref, self.local_ref.at[0])
        copy.start()
        copy.wait()

    @staticmethod
    def buffers(depth, rows, columns):
        half = rows // 2
        main = (half - UNIT) // 4
        return [
            pltpu.VMEM((depth, half, columns), BF16),
            pltpu.VMEM((2, half, columns), BF16),
            pltpu.VMEM((depth, 2 * main + UNIT, columns), BF16),
            pltpu.VMEM((depth, main + UNIT, columns), BF16),
            pltpu.VMEM((depth - 1, main + UNIT, columns), BF16),
            pltpu.VMEM((main + UNIT, columns), BF16),
        ]


def semaphores(local):
    return [
        pltpu.SemaphoreType.DMA((SEMAPHORES,)),
        pltpu.SemaphoreType.DMA((SEMAPHORES,)),
        pltpu.SemaphoreType.DMA((local,)),
    ]


def settings(limit, identity):
    return pltpu.CompilerParams(
        vmem_limit_bytes=limit * MIB, collective_id=identity, has_side_effects=True
    )


class Small:
    def __init__(self, here, links, small_ref, all_ref):
        self.here, self.links = here, links
        self.small_ref, self.all_ref = small_ref, all_ref
        self.slots = [links.slot() for _ in range(1, here.depth)]

    def copy(self, step, landing):
        target = self.all_ref.at[landing]
        return self.links.copy(self.slots[step - 1], self.small_ref, target, self.here.line(step))

    def start(self):
        self.all_ref[self.here.z] = self.small_ref[...]
        for step in range(1, self.here.depth):
            self.copy(step, self.here.z).start()

    def wait(self):
        for step in range(1, self.here.depth):
            self.copy(step, self.here.from_line(step)).wait()


def sum_small(here, links, small_ref, line_ref, plane_ref, result_ref):
    copies = []
    for step in range(1, here.depth):
        device = here.line(step)
        copy = links.copy(links.slot(), small_ref.at[device[0]], line_ref.at[step - 1], device)
        copy.start()
        copies.append(copy)
    total = small_ref[here.z]
    for step, copy in enumerate(copies):
        copy.wait()
        total += line_ref[step]
    plane_ref[here.j] = total
    copies = []
    for flip in range(1, 8):
        slot = links.slot()
        own = plane_ref.at[here.j]
        links.copy(slot, own, own, here.plane(flip)).start()
        other = plane_ref.at[here.near(flip)]
        copies.append(links.copy(slot, own, other, here.plane(flip)))
    for copy in copies:
        copy.wait()
    total = plane_ref[0]
    for other in range(1, 8):
        total += plane_ref[other]
    result_ref[...] = total


def open_kernel(first_count, *refs):
    count = first_count
    shards, (tokens_ref, small_ref) = refs[: count + 1], refs[count + 1 : count + 3]
    fulls = refs[count + 3 : 2 * count + 4]
    image_ref, all_ref, send_ref, recv_ref, local_ref = refs[2 * count + 4 :]
    here = Place()
    here.greet(range(1, 8), True)
    links = Links(send_ref, recv_ref)
    small = Small(here, links, small_ref, all_ref)
    swap = Swap(here, links, tokens_ref, image_ref, local_ref.at[0])
    qkv, *others = [Gather(here, links, shard, full) for shard, full in zip(shards, fulls)]
    small.start()
    qkv.line()
    swap.start()
    qkv.wait_line()
    qkv.sides()
    for other in others:
        other.line()
    qkv.corner()
    qkv.core()
    small.wait()
    swap.wait()
    qkv.end()
    for other in others:
        other.end_line()


def open_all(tokens, small, shards):
    depth = lax.axis_size("dp")
    vmem = pl.BlockSpec(memory_space=pltpu.VMEM)
    return pl.pallas_call(
        functools.partial(open_kernel, len(shards) - 1),
        in_specs=[ANY] * (len(shards) + 1) + [vmem],
        out_specs=[ANY] * (len(shards) + 1) + [vmem],
        out_shape=[
            shape_of((shard.shape[0] * depth, shard.shape[1]), shard.dtype) for shard in shards
        ]
        + [shape_of(tokens.shape, tokens.dtype), shape_of((depth, *small.shape), small.dtype)],
        scratch_shapes=semaphores(1),
        compiler_params=settings(62, 0),
        name="open_all",
    )(*shards, tokens, small)


def heads_of(values, head):
    return values[head * HEAD_DIM : (head + 1) * HEAD_DIM]


def attend_pair(queries, keys, values, mask, raised_ref, context_ref, inverse_ref):
    tokens = queries.shape[1]
    chunk = 256
    queries, keys, values = (part.astype(F32) for part in (queries, keys, values))
    for head in range(2):
        keys_t = jnp.concatenate([heads_of(keys, head), mask], axis=0)
        keys_h = keys_t.T.astype(BF16)
        ones = jnp.ones((8, tokens), F32)
        queries_t = jnp.concatenate([heads_of(queries, head), ones], axis=0).astype(BF16)
        values_t = heads_of(values, head).astype(BF16)
        for c in range(tokens // chunk):
            at = slice(c * chunk, (c + 1) * chunk)
            scores = mm(keys_h, queries_t[:, at], NN)
            peak = jnp.max(scores, axis=0, keepdims=True)
            raised = jnp.exp2((scores - peak) * (SCALE * LOG2_E))
            inverse = 1.0 / jnp.sum(raised, axis=0, keepdims=True)
            low = raised.astype(BF16)
            raised_ref[head, :, at] = low
            inverse_ref[0, head : head + 1, at] = inverse
            context = mm(values_t, low, NN) * inverse
            context_ref[head * HEAD_DIM : (head + 1) * HEAD_DIM, at] = context


def forward_kernel(blocks, pairs, *refs):
    x_ref, gain_ref, shift_ref, weight_ref, bias_ref, mask_ref = refs[:6]
    cot_ref, expand_ref, contract_ref = refs[6:9]
    packed_ref, normed_t_ref, raised_ref, context_ref, inverse_ref = refs[12:17]
    upstream_ref, output_full, expand_a, contract_a, expand_b, contract_b = refs[17:23]
    send_ref, recv_ref, local_ref = refs[23:]
    step = pl.program_id(0)
    here = Place()
    links = Links(send_ref, recv_ref)
    swap = Swap(here, links, cot_ref, upstream_ref, local_ref.at[0])
    now = [Gather(here, links, None, full) for full in (output_full, expand_a, contract_a)]
    later = [
        Gather(here, links, expand_ref, expand_b),
        Gather(here, links, contract_ref, contract_b),
    ]
    at_step(0, lambda: here.greet(range(1, 8), True))
    at_step(0, *[gather.sides for gather in now], *[gather.line for gather in later], swap.start)
    at_step(blocks + 2, *[gather.corner for gather in now])
    at_step(blocks + 5, *[gather.core for gather in now])

    rows = 128
    tokens, width = x_ref.shape
    columns = weight_ref.shape[1]

    @pl.when(step == 0)
    def _():
        def part(i, carry):
            at = pl.ds(pl.multiple_of(i * rows, rows), rows)
            hat, _ = centred(x_ref[at, :].astype(F32))
            normed = (hat * gain_ref[...] + shift_ref[...]).astype(BF16)
            normed_t_ref[:, at] = normed.T
            return carry

        lax.fori_loop(0, tokens // rows, part, 0)

    @pl.when(step < blocks)
    def _():
        prod = mm(weight_ref[...], normed_t_ref[...], TN)
        at = pl.ds(pl.multiple_of(step * columns, columns), columns)
        packed_ref[at, :] = (prod + bias_ref[...]).astype(BF16)

    @pl.when(step >= blocks)
    def _():
        pair = 2 * HEAD_DIM
        start = (step - blocks) * pair
        queries, keys, values = (
            packed_ref[pl.ds(pl.multiple_of(start + i * width, UNIT), pair), :] for i in range(3)
        )
        attend_pair(
            queries, keys, values, mask_ref[...], raised_ref, context_ref, inverse_ref
        )

    at_step(
        blocks + pairs - 1,
        swap.wait,
        *[gather.end for gather in now],
        *[gather.end_line for gather in later],
    )


def forward_image(x, gain, shift, weight, bias, mask_rows, cot, shards, fulls):
    tokens, width = x.shape
    total = weight.shape[1]
    step = 384
    pair = 2 * HEAD_DIM
    pairs = width // pair
    blocks = total // step
    depth = lax.axis_size("dp")

    def early(i):
        return jnp.minimum(i, blocks - 1)

    def late(i):
        return jnp.maximum(i - blocks, 0)

    return pl.pallas_call(
        functools.partial(forward_kernel, blocks, pairs),
        grid=(blocks + pairs,),
        in_specs=[
            whole((tokens, width)),
            whole((1, width)),
            whole((1, width)),
            pl.BlockSpec((width, step), lambda i: (0, early(i))),
            pl.BlockSpec((step, 1), lambda i: (early(i), 0)),
            whole((8, tokens)),
        ]
        + [ANY] * 6,
        out_specs=[
            whole((total, tokens)),
            whole((width, tokens)),
            pl.BlockSpec((2, tokens, tokens), lambda i: (late(i), 0, 0)),
            pl.BlockSpec((pair, tokens), lambda i: (late(i), 0)),
            pl.BlockSpec((1, 2, tokens), lambda i: (late(i), 0, 0)),
        ]
        + [ANY] * 6,
        out_shape=[
            shape_of((total, tokens), BF16),
            shape_of((width, tokens), BF16),
            shape_of((2 * pairs, tokens, tokens), BF16),
            shape_of((width, tokens), F32),
            shape_of((pairs, 2, tokens), F32),
            shape_of(cot.shape, cot.dtype),
        ]
        + [shape_of(full.shape, full.dtype) for full in fulls]
        + [shape_of((shard.shape[0] * depth, shard.shape[1]), BF16) for shard in shards],
        scratch_shapes=semaphores(1),
        input_output_aliases={9: 6, 10: 7, 11: 8},
        compiler_params=settings(56, 1),
        name="forward_image",
    )(x, gain, shift, weight, bias, mask_rows, cot, *shards, *fulls)


def join_kernel(x_ref, context_ref, weight_ref, bias_ref, gain_ref, shift_ref, middle_ref, normed_ref):
    branch = mm(context_ref[...].astype(BF16), weight_ref[...], TN)
    middle = x_ref[...].astype(F32) + (branch + bias_ref[...])
    middle_ref[...] = middle
    hat, _ = centred(middle)
    normed_ref[...] = (hat * gain_ref[...] + shift_ref[...]).astype(BF16)


def join_forward(x, context_t, weight, bias, gain, shift):
    tokens, width = x.shape
    step = 256
    rows = pl.BlockSpec((step, width), lambda i: (i, 0))
    return pl.pallas_call(
        join_kernel,
        grid=(tokens // step,),
        in_specs=[
            rows,
            pl.BlockSpec((width, step), lambda i: (0, i)),
            whole((width, width)),
            whole((1, width)),
            whole((1, width)),
            whole((1, width)),
        ],
        out_specs=[rows] * 2,
        out_shape=[shape_of((tokens, width), F32), shape_of((tokens, width), BF16)],
        compiler_params=pltpu.CompilerParams(vmem_limit_bytes=48 * MIB),
        name="join_forward",
    )(x, context_t, weight, bias, gain, shift)


def mlp_block(columns, refs, grads, accumulators):
    normed_ref, cot_ref, expand_ref, contract_ref, bias_ref, normed_t_ref, cot_t_ref = refs
    expand_grad_ref, contract_grad_ref, bias_grad_ref = grads
    out_acc_ref, back_acc_ref = accumulators
    block = expand_ref.shape[1]
    column = lax.broadcasted_iota(jnp.int32, (1, block), 1) + pl.program_id(0) * block
    kept = column < columns
    expand = jnp.where(kept, expand_ref[...], jnp.zeros((), BF16))
    contract = jnp.where(kept, contract_ref[...], jnp.zeros((), BF16))
    bias = jnp.where(kept, bias_ref[...], 0.0)
    hidden = mm(normed_ref[...], expand, NN) + bias
    act_grad = mm(cot_ref[...], contract, NN)
    square = hidden * hidden
    tanh = jnp.tanh(hidden * (GELU_COEF + (GELU_COEF * 0.044715) * square))
    half = 0.5 + 0.5 * tanh
    activated = (hidden * half).astype(BF16)
    slope = half + (0.5 * hidden) * (1.0 - tanh * tanh) * (
        GELU_COEF + (3 * 0.044715 * GELU_COEF) * square
    )
    pre_low = (act_grad * slope).astype(BF16)
    bias_grad_ref[...] = jnp.sum(pre_low.astype(F32), axis=0, keepdims=True)
    out_acc_ref[...] += mm(activated, contract, NT)
    contract_grad_ref[...] = mm(cot_t_ref[...], activated, NN).astype(BF16)
    expand_grad_ref[...] = mm(normed_t_ref[...], pre_low, NN).astype(BF16)
    back_acc_ref[...] += mm(pre_low, expand, NT)


def first_kernel(columns, last, *refs):
    normed_ref, cot_ref, expand_ref, contract_ref, bias_ref = refs[:5]
    grads, (out_acc_ref, back_acc_ref, normed_t_ref, cot_t_ref) = refs[7:10], refs[10:14]
    expand_b, contract_b, send_ref, recv_ref = refs[14:18]
    here = Place()
    links = Links(send_ref, recv_ref)
    gathers = [Gather(here, links, None, full) for full in (expand_b, contract_b)]
    at_step(0, lambda: here.greet((1, 2, 4), False), *[gather.sides for gather in gathers])
    at_step(5, *[gather.corner for gather in gathers])
    at_step(7, *[gather.core for gather in gathers])
    tokens, width = normed_ref.shape
    rows = 128

    @pl.when(pl.program_id(0) == 0)
    def _():
        def part(i, carry):
            at = pl.ds(pl.multiple_of(i * rows, rows), rows)
            normed_t_ref[:, at] = normed_ref[at, :].T
            cot_t_ref[:, at] = cot_ref[at, :].T
            out_acc_ref[at, :] = jnp.zeros((rows, width), F32)
            back_acc_ref[at, :] = jnp.zeros((rows, width), F32)
            return carry

        lax.fori_loop(0, tokens // rows, part, 0)

    refs = (normed_ref, cot_ref, expand_ref, contract_ref, bias_ref, normed_t_ref, cot_t_ref)
    mlp_block(columns, refs, grads, (out_acc_ref, back_acc_ref))
    at_step(last, *[gather.end for gather in gathers])


def mlp_first(normed, cot, expand, contract, bias, fulls):
    tokens, width = normed.shape
    columns = expand.shape[1]
    block = 256
    steps = -(-columns // block)
    slab = pl.BlockSpec((width, block), lambda i: (0, i))
    row = pl.BlockSpec((1, block), lambda i: (0, i))
    return pl.pallas_call(
        functools.partial(first_kernel, columns, steps - 1),
        grid=(steps,),
        in_specs=[whole((tokens, width))] * 2 + [slab, slab, row, ANY, ANY],
        out_specs=[slab, slab, row]
        + [whole((tokens, width))] * 2
        + [whole((width, tokens))] * 2
        + [ANY, ANY],
        out_shape=[shape_of((width, columns), BF16)] * 2
        + [shape_of((1, columns), F32)]
        + [shape_of((tokens, width), F32)] * 2
        + [shape_of((width, tokens), BF16)] * 2
        + [shape_of(full.shape, full.dtype) for full in fulls],
        scratch_shapes=semaphores(1)[:2],
        input_output_aliases={5: 7, 6: 8},
        compiler_params=settings(60, 2),
        name="mlp_first",
    )(normed, cot, expand, contract, bias, *fulls)


def second_kernel(columns, last, *refs):
    normed_ref, cot_ref, expand_ref, contract_ref, bias_ref, normed_t_ref, cot_t_ref = refs[:7]
    out_in, back_in, middle_ref, contract_bias_ref, gain_ref, expand_a, contract_a = refs[7:14]
    grads, (out_ref, middle_grad_ref, sums_ref) = refs[14:17], refs[17:20]
    states, (send_ref, recv_ref, local_ref, out_acc_ref, back_acc_ref) = refs[20:22], refs[22:27]
    buffers = refs[27:]
    here = Place()
    links = Links(send_ref, recv_ref)
    sums = [
        Reduce(here, links, (*buffers[3 * i : 3 * i + 3], None, None, None), local_ref.at[pl.ds(4 * i, 4)], grad)
        for i, grad in enumerate((expand_a, contract_a))
    ]
    tokens, width = normed_ref.shape
    rows = 128

    def load():
        copies = [
            pltpu.make_async_copy(source, target, local_ref.at[8 + i])
            for i, (source, target) in enumerate(((out_in, out_acc_ref), (back_in, back_acc_ref)))
        ]
        for copy in copies:
            copy.start()
        for copy in copies:
            copy.wait()

    at_step(0, lambda: here.greet((1, 2, 4), False), *[one.pair for one in sums], load)
    at_step(2, *[one.sides for one in sums])
    refs = (normed_ref, cot_ref, expand_ref, contract_ref, bias_ref, normed_t_ref, cot_t_ref)
    mlp_block(columns, refs, grads, (out_acc_ref, back_acc_ref))

    @pl.when(pl.program_id(0) == last)
    def _():
        def part(i, sums):
            at = pl.ds(pl.multiple_of(i * rows, rows), rows)
            middle = middle_ref[at, :]
            cot = cot_ref[at, :].astype(F32)
            out_ref[at, :] = (middle + (out_acc_ref[at, :] + contract_bias_ref[...])).astype(BF16)
            hat, rate = centred(middle)
            grad = back_acc_ref[at, :]
            scaled = grad * gain_ref[...]
            mean_one = jnp.mean(scaled, axis=-1, keepdims=True)
            mean_two = jnp.mean(scaled * hat, axis=-1, keepdims=True)
            middle_grad = cot + rate * (scaled - mean_one - hat * mean_two)
            middle_grad_ref[at, :] = middle_grad
            low = middle_grad.astype(BF16).astype(F32)
            terms = (grad * hat, grad, low, cot)
            return tuple(
                total + jnp.sum(term, axis=0, keepdims=True) for total, term in zip(sums, terms)
            )

        zero = jnp.zeros((1, width), F32)
        totals = lax.fori_loop(0, tokens // rows, part, (zero,) * 4)
        for place, total in enumerate(totals):
            sums_ref[place : place + 1, :] = total
        for one in sums:
            one.wait_sides()
        for one, state in zip(sums, states):
            one.save(state)
            one.finish()


def mlp_second(normed, cot, expand, contract, bias, carried, middle, contract_bias, gain, grads):
    tokens, width = normed.shape
    columns = expand.shape[1]
    block = 256
    steps = -(-columns // block)
    depth = lax.axis_size("dp")
    rows = width // depth
    slab = pl.BlockSpec((width, block), lambda i: (0, i))
    row = pl.BlockSpec((1, block), lambda i: (0, i))
    buffers = [Reduce.buffers(depth, rows, grad.shape[1])[:3] for grad in grads]
    out_acc, back_acc, normed_t, cot_t = carried
    return pl.pallas_call(
        functools.partial(second_kernel, columns, steps - 1),
        grid=(steps,),
        in_specs=[whole((tokens, width))] * 2
        + [slab, slab, row]
        + [whole((width, tokens))] * 2
        + [ANY, ANY, whole((tokens, width)), whole((1, width)), whole((1, width)), ANY, ANY],
        out_specs=[slab, slab, row]
        + [whole((tokens, width))] * 2
        + [whole((8, width)), ANY, ANY],
        out_shape=[shape_of((width, columns), BF16)] * 2
        + [shape_of((1, columns), F32)]
        + [
            shape_of((tokens, width), BF16),
            shape_of((tokens, width), F32),
            shape_of((8, width), F32),
        ]
        + [shape_of((depth, rows // 2, grad.shape[1]), BF16) for grad in grads],
        scratch_shapes=semaphores(10)
        + [pltpu.VMEM((tokens, width), F32)] * 2
        + buffers[0]
        + buffers[1],
        compiler_params=settings(62, 3),
        name="mlp_second",
    )(
        normed, cot, expand, contract, bias, normed_t, cot_t, out_acc, back_acc, middle,
        contract_bias, gain, *grads,
    )


def attend_pair_back(queries, keys, values, grads, context_ref, inverse_ref, raised_ref, result_ref):
    tokens = queries.shape[1]
    chunk = 256
    queries, keys, values, grads = (
        part.astype(F32) for part in (queries, keys, values, grads)
    )
    for head in range(2):
        span = slice(head * HEAD_DIM, (head + 1) * HEAD_DIM)
        keys_t = heads_of(keys, head).astype(BF16)
        queries_t = heads_of(queries, head).astype(BF16)
        values_h = heads_of(values, head).T.astype(BF16)
        grad_low = (heads_of(grads, head) * inverse_ref[0, head : head + 1, :]).astype(BF16)
        drop = jnp.sum(grad_low.astype(F32) * context_ref[span, :], axis=0, keepdims=True)
        key_grad = jnp.zeros((HEAD_DIM, tokens), F32)
        value_grad = jnp.zeros((HEAD_DIM, tokens), F32)
        for c in range(tokens // chunk):
            at = slice(c * chunk, (c + 1) * chunk)
            raised = raised_ref[head, :, at]
            prob_grad = mm(values_h, grad_low[:, at], NN)
            score = (raised.astype(F32) * (prob_grad - drop[:, at])).astype(BF16)
            result_ref[0, span, at] = (mm(keys_t, score, NN) * SCALE).astype(BF16)
            key_grad += mm(queries_t[:, at], score, NT)
            value_grad += mm(grad_low[:, at], raised, NT)
        result_ref[1, span, :] = (key_grad * SCALE).astype(BF16)
        result_ref[2, span, :] = value_grad.astype(BF16)


def back_kernel(blocks, pairs, *refs):
    middle_grad_ref, context_col_ref, weight_ref, q_ref, k_ref, v_ref = refs[:6]
    context_ref, inverse_ref, raised_ref = refs[6:9]
    states, new_grads = refs[9:11], refs[11:13]
    packed_grad_ref, weight_grad_ref = refs[13:15]
    results, new_states = refs[15:17], refs[17:19]
    send_ref, recv_ref, local_ref, grad_t_ref, total_ref = refs[19:24]
    buffers = refs[24:]
    step = pl.program_id(0)
    here = Place()
    links = Links(send_ref, recv_ref)
    old = [
        Reduce(
            here,
            links,
            (buffers[4 * i], None, None, *buffers[4 * i + 1 : 4 * i + 4]),
            local_ref.at[pl.ds(2 * i, 2)],
            None,
            results[i],
        )
        for i in range(2)
    ]
    new = [
        Reduce(
            here,
            links,
            (*buffers[8 + 4 * i : 12 + 4 * i], None, None),
            local_ref.at[pl.ds(4 + 4 * i, 4)],
            new_grads[i],
        )
        for i in range(2)
    ]

    def resume():
        for one, state in zip(old, states):
            one.load(state)
        for one in old:
            one.begin(one.start_next)

    at_step(0, lambda: here.greet((1, 2, 4), True), *[one.pair for one in new], resume)
    at_step(blocks, *[one.sides for one in new], *[one.after_next for one in old])
    at_step(blocks + 5, *[one.after_sides for one in new], *[one.after_line for one in old])
    at_step(blocks + 6, *[one.corner for one in old])
    at_step(blocks + 7, *[one.core for one in old])

    @pl.when(step < blocks)
    def _():
        low = middle_grad_ref[...].astype(BF16)
        columns = low.shape[0]
        at = pl.ds(pl.multiple_of(step * columns, columns), columns)
        grad_t_ref[:, at] = mm(weight_ref[...], low, NT).astype(BF16)
        part = mm(context_col_ref[...].astype(BF16), low, NN)

        @pl.when(step == 0)
        def _():
            total_ref[...] = part

        @pl.when(step > 0)
        def _():
            total_ref[...] += part

        @pl.when(step == blocks - 1)
        def _():
            weight_grad_ref[...] = total_ref[...].astype(BF16)

    @pl.when(step >= blocks)
    def _():
        pair = 2 * HEAD_DIM
        start = pl.multiple_of((step - blocks) * pair, UNIT)
        grads = grad_t_ref[pl.ds(start, pair), :]
        attend_pair_back(
            q_ref[...], k_ref[...], v_ref[...], grads,
            context_ref, inverse_ref, raised_ref, packed_grad_ref,
        )

    def end():
        for one in new:
            one.wait_next()
        for one, state in zip(new, new_states):
            one.save(state)
            one.finish()
        for one in old:
            one.end()

    at_step(blocks + pairs - 1, end)


def back_image(middle_grad, context_t, weight, packed, inverse, raised, states, new_grads):
    total, tokens = packed.shape
    width = total // 3
    pair = 2 * HEAD_DIM
    pairs = width // pair
    step = 256
    blocks = tokens // step
    depth = lax.axis_size("dp")
    rows = width // depth

    def early(i):
        return jnp.minimum(i, blocks - 1)

    def late(i):
        return jnp.maximum(i - blocks, 0)

    def pair_at(first):
        return pl.BlockSpec((pair, tokens), lambda i: (late(i) + first, 0))

    buffers = []
    for state in states:
        made = Reduce.buffers(depth, rows, state.shape[2])
        buffers += [made[0], *made[3:]]
    for grad in new_grads:
        buffers += Reduce.buffers(depth, rows, grad.shape[1])[:4]
    return pl.pallas_call(
        functools.partial(back_kernel, blocks, pairs),
        grid=(blocks + pairs,),
        in_specs=[
            pl.BlockSpec((step, width), lambda i: (early(i), 0)),
            pl.BlockSpec((width, step), lambda i: (0, early(i))),
            whole((width, width)),
            pair_at(0),
            pair_at(pairs),
            pair_at(2 * pairs),
            pair_at(0),
            pl.BlockSpec((1, 2, tokens), lambda i: (late(i), 0, 0)),
            pl.BlockSpec((2, tokens, tokens), lambda i: (late(i), 0, 0)),
        ]
        + [ANY] * 4,
        out_specs=[
            pl.BlockSpec((3, pair, tokens), lambda i: (0, late(i), 0)),
            whole((width, width)),
        ]
        + [ANY] * 4,
        out_shape=[shape_of((3, width, tokens), BF16), shape_of((width, width), BF16)]
        + [shape_of((rows, state.shape[2]), BF16) for state in states]
        + [shape_of((depth, rows // 2, grad.shape[1]), BF16) for grad in new_grads],
        scratch_shapes=semaphores(12)
        + [pltpu.VMEM((width, tokens), BF16), pltpu.VMEM((width, width), F32)]
        + buffers,
        compiler_params=settings(62, 4),
        name="back_image",
    )(middle_grad, context_t, weight, packed, packed, packed, context_t, inverse, raised,
      *states, *new_grads)


def input_kernel(last, *refs):
    normed_t_ref, packed_grad_ref, weight_ref, x_ref, middle_grad_ref, gain_ref = refs[:6]
    states, (output_grad_ref, out_ref) = refs[6:8], refs[8:10]
    input_grad_ref, weight_grad_ref, bias_grad_ref, sums_ref = refs[10:14]
    results, output_result, layer_ref = refs[14:16], refs[16], refs[17]
    send_ref, recv_ref, local_ref, back_ref = refs[18:22]
    buffers = refs[22:]
    index = pl.program_id(0)
    here = Place()
    links = Links(send_ref, recv_ref)
    old = [
        Reduce(
            here,
            links,
            (buffers[3 * i], None, None, None, *buffers[3 * i + 1 : 3 * i + 3]),
            local_ref.at[pl.ds(2 * i, 2)],
            None,
            results[i],
        )
        for i in range(2)
    ]
    new = Reduce(here, links, buffers[6:], local_ref.at[pl.ds(4, 4)], output_grad_ref, output_result)
    swap = Swap(here, links, out_ref, layer_ref, local_ref.at[8])

    def resume():
        for one, state in zip(old, states):
            one.load(state)
        for one in old:
            one.begin(one.start_line)

    at_step(0, lambda: here.greet(range(1, 8), True), new.pair, resume)
    at_step(1, new.sides, swap.start)
    at_step(4, new.after_sides)
    at_step(6, new.after_next, *[one.after_line for one in old])
    at_step(7, *[one.corner for one in old], new.after_line)
    at_step(8, *[one.core for one in old], new.corner)

    tokens, width = x_ref.shape
    rows = 128
    packed_grad = packed_grad_ref[...]
    weight_grad_ref[...] = mm(normed_t_ref[...], packed_grad, NT).astype(BF16)
    bias_grad_ref[...] = jnp.sum(packed_grad.astype(F32), axis=1, keepdims=True)
    part = mm(weight_ref[...], packed_grad, NN)

    @pl.when(index == 0)
    def _():
        back_ref[...] = part

    @pl.when(index > 0)
    def _():
        back_ref[...] += part

    @pl.when(index == last)
    def _():
        def part_of(i, sums):
            at = pl.ds(pl.multiple_of(i * rows, rows), rows)
            hat, rate = centred(x_ref[at, :].astype(F32))
            grad = back_ref[:, at].T
            scaled = grad * gain_ref[...]
            mean_one = jnp.mean(scaled, axis=-1, keepdims=True)
            mean_two = jnp.mean(scaled * hat, axis=-1, keepdims=True)
            result = middle_grad_ref[at, :] + rate * (scaled - mean_one - hat * mean_two)
            input_grad_ref[at, :] = result.astype(BF16)
            terms = (grad * hat, grad)
            return tuple(
                total + jnp.sum(term, axis=0, keepdims=True) for total, term in zip(sums, terms)
            )

        zero = jnp.zeros((1, width), F32)
        totals = lax.fori_loop(0, tokens // rows, part_of, (zero,) * 2)
        for place, total in enumerate(totals):
            sums_ref[place : place + 1, :] = total
        new.core()
        for one in old:
            one.end()
        new.end()
        swap.wait()


def input_back(normed_t, packed_grad, weight, x, middle_grad, gain, states, output_grad, out):
    tokens, width = x.shape
    total = weight.shape[1]
    step = 384
    depth = lax.axis_size("dp")
    rows = width // depth
    buffers = []
    for state in states:
        made = Reduce.buffers(depth, rows, state.shape[2])
        buffers += [made[0], *made[4:]]
    buffers += Reduce.buffers(depth, rows, output_grad.shape[1])
    return pl.pallas_call(
        functools.partial(input_kernel, total // step - 1),
        grid=(total // step,),
        in_specs=[
            whole((width, tokens)),
            pl.BlockSpec((step, tokens), lambda i: (i, 0)),
            pl.BlockSpec((width, step), lambda i: (0, i)),
            whole((tokens, width)),
            whole((tokens, width)),
            whole((1, width)),
        ]
        + [ANY] * 4,
        out_specs=[
            whole((tokens, width)),
            pl.BlockSpec((width, step), lambda i: (0, i)),
            pl.BlockSpec((step, 1), lambda i: (i, 0)),
            whole((8, width)),
        ]
        + [ANY] * 4,
        out_shape=[
            shape_of((tokens, width), BF16),
            shape_of((width, total), BF16),
            shape_of((total, 1), F32),
            shape_of((8, width), F32),
        ]
        + [shape_of((rows, state.shape[2]), BF16) for state in states]
        + [shape_of((rows, output_grad.shape[1]), BF16), shape_of(out.shape, out.dtype)],
        scratch_shapes=semaphores(9) + [pltpu.VMEM((width, tokens), F32)] + buffers,
        compiler_params=settings(60, 5),
        name="input_back",
    )(normed_t, packed_grad, weight, x, middle_grad, gain, *states, output_grad, out)


def close_kernel(grad_ref, small_ref, back_ref, result_ref, sum_ref, input_ref, *scratch):
    send_ref, recv_ref, local_ref, line_ref, plane_ref = scratch[:5]
    here = Place()
    here.greet(range(1, 8), True)
    links = Links(send_ref, recv_ref)
    one = Reduce(here, links, scratch[5:], local_ref.at[pl.ds(0, 4)], grad_ref, result_ref)
    swap = Swap(here, links, back_ref, input_ref, local_ref.at[4])
    one.pair()
    one.sides()
    one.after_sides()
    swap.start()
    one.after_next()
    sum_small(here, links, small_ref, line_ref, plane_ref, sum_ref)
    one.after_line()
    one.corner()
    one.core()
    one.end()
    swap.wait()


def close_all(grad, small, back):
    depth = lax.axis_size("dp")
    rows = grad.shape[0] // depth
    vmem = pl.BlockSpec(memory_space=pltpu.VMEM)
    return pl.pallas_call(
        close_kernel,
        in_specs=[ANY, vmem, ANY],
        out_specs=[ANY, vmem, ANY],
        out_shape=[
            shape_of((rows, grad.shape[1]), grad.dtype),
            shape_of(small.shape[1:], small.dtype),
            shape_of(back.shape, back.dtype),
        ],
        scratch_shapes=semaphores(5)
        + [
            pltpu.VMEM((depth - 1, *small.shape[1:]), F32),
            pltpu.VMEM((8, *small.shape[1:]), F32),
        ]
        + Reduce.buffers(depth, rows, grad.shape[1]),
        compiler_params=settings(60, 6),
        name="close_all",
    )(grad, small, back)


def shards_image(
    tokens,
    key_mask,
    cotangent,
    qkv_weight,
    output_weight,
    expand_weight,
    contract_weight,
    norm1_gain,
    norm1_bias,
    query_bias,
    value_bias,
    output_bias,
    norm2_gain,
    norm2_bias,
    expand_bias,
    contract_bias,
):
    images_here, slice_len, width = tokens.shape
    length = slice_len * lax.axis_size("seq")
    depth = lax.axis_size("dp")
    vectors = (
        norm1_gain,
        norm1_bias,
        query_bias,
        value_bias,
        output_bias,
        norm2_gain,
        norm2_bias,
        expand_bias,
        contract_bias,
    )
    sizes = [vector.shape[0] for vector in vectors]
    block = 16 * 128
    padded = -(-sum(sizes) // block) * block
    joined = jnp.pad(jnp.concatenate(vectors), (0, padded - sum(sizes))).reshape(-1, 128)
    cut = -(-expand_weight.shape[1] // 512) * 256
    expand_a, expand_b = expand_weight[:, :cut], expand_weight[:, cut:]
    contract_a, contract_b = contract_weight[:, :cut], contract_weight[:, cut:]

    qkv_full, *fulls, image, joined = open_all(
        tokens, joined, (qkv_weight, output_weight, expand_a, contract_a)
    )
    image = image.reshape(length, width)
    joined = joined.reshape(depth, padded)
    full = []
    start = 0
    for size in sizes:
        full.append(joined[:, start : start + size].reshape(1, -1).astype(F32))
        start += size
    gain_one, shift_one, bias_q, bias_v, bias_out, gain_two, shift_two, bias_up, bias_down = full
    bias_three = jnp.concatenate([bias_q, jnp.zeros_like(bias_q), bias_v], axis=1).reshape(-1, 1)
    mask_row = lax.dynamic_slice_in_dim(key_mask, lax.axis_index("seq"), 1, 0)
    masked = jnp.where(mask_row > 0, 0.0, NEGATIVE)
    mask_rows = jnp.concatenate([masked, jnp.zeros((7, length), F32)], axis=0)

    packed, normed_t, raised, context_t, inverse, upstream, *fulls = forward_image(
        image, gain_one, shift_one, qkv_full, bias_three, mask_rows, cotangent,
        (expand_b, contract_b), fulls,
    )
    output_full, expand_one, contract_one, *fulls = fulls
    upstream = upstream.reshape(length, width)
    middle, normed_two = join_forward(
        image, context_t, output_full, bias_out, gain_two, shift_two
    )
    expand_grad, contract_grad, up_one, *carried, expand_two, contract_two = mlp_first(
        normed_two, upstream, expand_one, contract_one, bias_up[:, :cut], fulls
    )
    *new_grads, up_two, out, middle_grad, sums_two, state_one, state_two = mlp_second(
        normed_two, upstream, expand_two, contract_two, bias_up[:, cut:], carried, middle,
        bias_down, gain_two, (expand_grad, contract_grad),
    )
    packed_grad, output_grad, expand_sum_a, contract_sum_a, state_one, state_two = back_image(
        middle_grad, context_t, output_full, packed, inverse, raised,
        (state_one, state_two), new_grads,
    )
    packed_grad = packed_grad.reshape(3 * width, length)
    (
        input_grad, qkv_grad, bias_grad, sums_one,
        expand_sum_b, contract_sum_b, output_sum, out,
    ) = input_back(
        normed_t, packed_grad, qkv_full, image, middle_grad, gain_one, (state_one, state_two),
        output_grad, out.reshape(images_here, slice_len, width),
    )

    bias_grad = bias_grad.reshape(3, width)
    small = (
        sums_one[0],
        sums_one[1],
        bias_grad[0],
        bias_grad[2],
        sums_two[2],
        sums_two[0],
        sums_two[1],
        jnp.concatenate([up_one[0], up_two[0]]),
        sums_two[3],
    )
    small = jnp.concatenate([part.reshape(depth, -1) for part in small], axis=1)
    small = jnp.pad(small, ((0, 0), (0, padded - sum(sizes)))).reshape(depth, -1, 128)
    qkv_sum, small, input_grad = close_all(
        qkv_grad, small, input_grad.reshape(images_here, slice_len, width)
    )
    small = small.reshape(-1)
    outs = []
    start = 0
    for size in sizes:
        outs.append(small[start : start + size])
        start += size
    return (
        out,
        input_grad,
        qkv_sum.astype(F32),
        output_sum.astype(F32),
        jnp.concatenate([expand_sum_a, expand_sum_b], axis=1).astype(F32),
        jnp.concatenate([contract_sum_a, contract_sum_b], axis=1).astype(F32),
        *outs,
    )


def solution(mesh):
    def apply(*arguments):
        images_here = arguments[0].shape[0] // mesh.shape["dp"]
        whole_images = images_here == mesh.shape["seq"]
        body = shards_image if whole_images else shards_general
        return jax.shard_map(
            body, mesh=mesh, in_specs=in_specs, out_specs=out_specs, check_vma=False
        )(*arguments)

    in_specs = (
        P("dp", "seq", None),
        P("dp", None),
        P("dp", "seq", None),
        P("dp", None),
        P("dp", None),
        P("dp", None),
        P("dp", None),
        P("dp"),
        P("dp"),
        P("dp"),
        P("dp"),
        P("dp"),
        P("dp"),
        P("dp"),
        P("dp"),
        P("dp"),
    )
    out_specs = (
        P("dp", "seq", None),
        P("dp", "seq", None),
        P("dp", None),
        P("dp", None),
        P("dp", None),
        P("dp", None),
        P("dp"),
        P("dp"),
        P("dp"),
        P("dp"),
        P("dp"),
        P("dp"),
        P("dp"),
        P("dp"),
        P("dp"),
    )
    return apply
```
